256 devices in a mesh: row: 16 (over z, core), col: 16 (over x, y).
Axes of the slice: x: 4, y: 4, z: 8, core: 2. Of those that a mesh axis runs over, the one named last changes fastest.
Arguments:
- activations: bfloat16 [512, 12288], P('col', 'row'), may hold values from -6 to 6
- output_grad: bfloat16 [512, 12288], P('col', 'row'), may hold values from -3 to 3
- up_weight: bfloat16 [12288, 24576], P('row', 'col'), may hold values from -0.0546875 to 0.0546875
- down_weight: bfloat16 [12288, 24576], P('row', 'col'), may hold values from -0.0390625 to 0.0390625
- up_bias: bfloat16 [24576], P('col'), may hold values from -4 to 4
Outputs:
- input_grad: bfloat16 [512, 12288], P('col', 'row')
- up_grad: bfloat16 [12288, 24576], P('row', 'col')
- down_grad: bfloat16 [12288, 24576], P('row', 'col')
- bias_grad: float32 [24576], P('col')
The draws below stay inside these ranges and needn't reach their ends.
All inputs are finite; a program needn't handle non-finite values.
Results may differ from the reference program's by a relative error of at most 0.0049.
Values may be sent and summed in bfloat16 or wider, within the bound.
A program may use at most 64 MiB of HBM per device.

```python
import jax
import jax.numpy as jnp
from jax import lax

D = 12288
F = 24576
TOKENS = 512


def with_spikes(entries, own_key, source, target, shards_of, factor):
    owner, partner = [(jnp.arange(entries.shape[axis_at]) // (entries.shape[axis_at] // shards_of)).reshape([-1 if axis == axis_at else 1 for axis in range(entries.ndim)]) for axis_at in (source, target)]
    chosen = jax.random.permutation(own_key, shards_of)[partner]
    strong = (owner == chosen) | (owner == (partner + shards_of // 2) % shards_of)
    return jnp.where(strong, factor * entries, entries)


def levels(stream_key, extent, pieces, low, high):
    loudness = 1.0
    for position, parts in pieces:
        heights = jax.random.uniform(jax.random.fold_in(jax.random.fold_in(stream_key, 6), position), (parts,), jnp.float32, low / len(pieces), high / len(pieces))
        loudness = loudness * jnp.repeat(jnp.exp(heights), extent[position] // parts).reshape((-1,) + (1,) * (len(extent) - 1 - position))
    return loudness


def scatter_about(key, shape, spread, most, pieces=(), dtype=jnp.bfloat16):
    drawn = jax.random.normal(key, shape, jnp.float32) * spread
    if len(pieces) > 0:
        drawn = levels(key, shape, pieces, -0.22, 0.18) * drawn
    return jnp.clip(drawn, min=-most, max=most).astype(dtype)


def gaussian_with(own_key, shape, deviation, limit, pieces, heavy, held_as=jnp.bfloat16):
    drawn = deviation * jax.random.normal(own_key, shape, jnp.float32)
    if pieces:
        drawn = drawn * levels(own_key, shape, pieces, -0.22, 0.18)
    return jnp.clip(with_spikes(drawn, jax.random.fold_in(own_key, 3), *heavy), -limit, limit).astype(held_as)


def setup_inputs(seed: int = 0) -> dict:
    seeds = jax.random.split(jax.random.key(seed), 6)
    return {
        "activations": gaussian_with(seeds[0], (TOKENS, D), 1.0, 6.0, ((0, 16), (1, 16)), (1, 0, 16, 2.0)),
        "output_grad": gaussian_with(seeds[1], (TOKENS, D), 0.5, 3.0, ((0, 16), (1, 16)), (1, 0, 16, 2.0)),
        "up_weight": scatter_about(seeds[2], (D, F), D ** -0.5, 0.0546875, ((0, 16), (1, 16))),
        "down_weight": scatter_about(seeds[3], (D, F), F ** -0.5, 0.0390625, ((0, 16), (1, 16))),
        "up_bias": scatter_about(seeds[4], (F,), 1.0, 4.0, ((0, 16),)),
    }


def gelu_parts(pre_act):
    coeff = 0.7978845608028654
    cubic = 0.044715
    inner = coeff * (pre_act + cubic * pre_act * pre_act * pre_act)
    tanh_val = jnp.tanh(inner)
    value = 0.5 * pre_act * (1.0 + tanh_val)
    slope = 0.5 * (1.0 + tanh_val) + 0.5 * pre_act * (1.0 - tanh_val * tanh_val) * coeff * (1.0 + 3.0 * cubic * pre_act * pre_act)
    return value, slope


def reference(activations, output_grad, up_weight, down_weight, up_bias):
    pre_act = jnp.dot(activations, up_weight, preferred_element_type=jnp.float32) + up_bias.astype(jnp.float32)
    hidden_grad = jnp.dot(output_grad, down_weight, preferred_element_type=jnp.float32)
    value, slope = gelu_parts(pre_act)
    act_grad = (hidden_grad * slope).astype(jnp.bfloat16)
    hidden_out = value.astype(jnp.bfloat16)
    up_grad = lax.dot_general(activations, act_grad, (((0,), (0,)), ((), ())), preferred_element_type=jnp.float32).astype(jnp.bfloat16)
    down_grad = lax.dot_general(output_grad, hidden_out, (((0,), (0,)), ((), ())), preferred_element_type=jnp.float32).astype(jnp.bfloat16)
    bias_grad = jnp.sum(act_grad.astype(jnp.float32), axis=0)
    input_grad = lax.dot_general(act_grad, up_weight, (((1,), (1,)), ((), ())), preferred_element_type=jnp.float32).astype(jnp.bfloat16)
    return (input_grad, up_grad, down_grad, bias_grad)
```

```python
import functools

import jax
import jax.numpy as jnp
from jax import lax
from jax.experimental import pallas as pl
from jax.experimental.pallas import tpu as pltpu
from jax.sharding import PartitionSpec as P

MESH = pl.DeviceIdType.MESH
F32 = jnp.float32
BF16 = jnp.bfloat16

NZ = 8
R = 16
H = 768
TILE = 256
N_SEM = 220
N_LOCAL = 32


def gelu_parts(pre_act):
    coeff = 0.7978845608028654
    cubic = 0.044715
    inner = coeff * (pre_act + cubic * pre_act * pre_act * pre_act)
    tanh_val = jnp.tanh(inner)
    value = 0.5 * pre_act * (1.0 + tanh_val)
    slope = 0.5 * (1.0 + tanh_val) + 0.5 * pre_act * (1.0 - tanh_val * tanh_val) * coeff * (
        1.0 + 3.0 * cubic * pre_act * pre_act
    )
    return (value, slope)


def enc(v):
    return (v * jnp.abs(v)).astype(BF16)


def dec(code):
    v = code.astype(F32)
    root = jnp.sqrt(jnp.abs(v))
    return jnp.where(v < 0, -root, root)


def exchange_kernel(
    act_hbm, og_hbm, wu_hbm, wd_hbm, bias_ref,
    g_out, xt_out, ig_out,
    x_buf, wx, wu_other, part, sp, rp, sm, rm, g_buf, xt, ig_acc,
    s1, r1, t1, s2, r2, send_sem, recv_sem, local_sem,
):
    row, col = lax.axis_index("row"), lax.axis_index("col")
    z, core = row // 2, row % 2
    x, y = col // 4, col % 4
    par, yh = y % 2, y // 2

    sib = (z * 2 + 1 - core, col)
    zp = (((z + 1) % NZ) * 2 + core, col)
    zm = (((z + NZ - 1) % NZ) * 2 + core, col)

    def xpeer(k):
        return (row, ((x + k) % 4) * 4 + y)

    def ypeer(k):
        return (row, x * 4 + (y + k) % 4)

    sent, local = [], []
    count = {"remote": 0, "local": 0}

    def remote(src, dst, device):
        i = count["remote"]
        count["remote"] = i + 1
        copy = pltpu.make_async_remote_copy(
            src_ref=src, dst_ref=dst, send_sem=send_sem.at[i], recv_sem=recv_sem.at[i],
            device_id=device, device_id_type=MESH,
        )
        copy.start()
        sent.append(copy)
        return copy

    def move(src, dst):
        i = count["local"]
        count["local"] = i + 1
        copy = pltpu.make_async_copy(src, dst, local_sem.at[i])
        copy.start()
        return copy

    own_cols = pl.ds(pl.multiple_of(core * H, H), H)
    other_cols = pl.ds(pl.multiple_of((1 - core) * H, H), H)

    def xi(arr, whose, h):
        return arr * 4 + whose * 2 + h

    mine = {}
    for h in range(2):
        for arr, src in ((0, act_hbm), (1, og_hbm)):
            mine[arr, h] = move(src.at[pl.ds(h * R, R)], x_buf.at[xi(arr, 0, h), par, x, yh])
    w_own = [
        move(wu_hbm.at[:, own_cols], wx.at[0]),
        move(wd_hbm.at[:, own_cols], wx.at[2]),
    ]
    w_oth = move(wu_hbm.at[:, other_cols], wu_other)

    barrier = pltpu.get_barrier_semaphore()
    peers = [sib, zp, zm] + [xpeer(k) for k in (1, 2, 3)] + [ypeer(k) for k in (1, 2, 3)]
    for peer in peers:
        pl.semaphore_signal(barrier, inc=1, device_id=peer, device_id_type=MESH)
    pl.semaphore_wait(barrier, len(peers))

    stage1, stage2, shared = {}, {}, {}

    def gather1(h):
        for arr in (0, 1):
            mine[arr, h].wait()
        for k in (1, 2, 3):
            for arr, peer in ((0, xpeer(k)), (1, ypeer(k))):
                slot = x_buf.at[xi(arr, 0, h), par, x, yh]
                stage1[arr, h, k] = remote(slot, slot, peer)

    def group(arr, whose, h, k):
        if arr == 0:
            yk = (y + 4 - k) % 4
            return x_buf.at[xi(0, whose, h), yk % 2, :, yk // 2]
        return x_buf.at[xi(1, whose, h), :, (x + 4 - k) % 4]

    def share(arr, h, k):
        shared[arr, h, k] = remote(group(arr, 0, h, k), group(arr, 1, h, k), sib)

    def gather2(h):
        for k in (1, 2, 3):
            for arr in (0, 1):
                stage1[arr, h, k].wait_recv()
        for k in (1, 2, 3):
            for arr, peer in ((0, ypeer(k)), (1, xpeer(k))):
                slot = group(arr, 0, h, 0)
                stage2[arr, h, k] = remote(slot, slot, peer)
        for arr in (0, 1):
            share(arr, h, 0)

    def gather3(h):
        for k in (1, 3, 2):
            for arr in (0, 1):
                stage2[arr, h, k].wait_recv()
                share(arr, h, k)

    def gathered(h):
        for k in (0, 1, 3, 2):
            for arr in (0, 1):
                shared[arr, h, k].wait_recv()

    def project(h):
        for ab in (0, 1):
            lhs = [x_buf[xi(ab, w, h)].reshape(256, H) for w in (0, 1)]

            @pl.loop(0, H // TILE)
            def _(n):
                cols = pl.ds(pl.multiple_of(n * TILE, TILE), TILE)
                total = jnp.dot(lhs[0], wx[ab * 2, :, cols], preferred_element_type=F32)
                total += jnp.dot(lhs[1], wx[ab * 2 + 1, :, cols], preferred_element_type=F32)
                part[h * 2 + ab, :, :, :, cols] = total.reshape(2, NZ, R, TILE)

    up, down = {}, {}

    def reduce_step(q, s):
        h, p = q // 2, q % 2
        for way, hops, send_buf, recv_buf, device, first in (
            (1, up, sp, rp, zp, 0),
            (-1, down, sm, rm, zm, 1),
        ):
            owner = (z + NZ + way * (4 - s)) % NZ
            if s > 0:
                hops[q, s - 1].wait_recv()
            for ab in (0, 1):
                if s == 0 and ab != first:
                    continue
                v = part[h * 2 + ab, p, owner]
                if s > 1 or (s == 1 and ab == first):
                    v = v + dec(recv_buf[q * 4 + s - 1, ab])
                send_buf[q * 4 + s, ab] = enc(v)
            which = pl.ds(first, 1) if s == 0 else pl.ds(0, 2)
            hops[q, s] = remote(
                send_buf.at[q * 4 + s, which], recv_buf.at[q * 4 + s, which], device
            )

    fwd, bwd, pair = {}, {}, {}

    def to_sibling(q, i, owner):
        pair[q, i] = remote(g_buf.at[pl.ds(0, 2), q, owner], g_buf.at[pl.ds(2, 2), q, owner], sib)

    def finish(q):
        h, p = q // 2, q % 2
        up[q, 3].wait_recv()
        down[q, 3].wait_recv()
        both = [
            part[h * 2 + ab, p, z] + dec(rp[q * 4 + 3, ab]) + dec(rm[q * 4 + 3, ab])
            for ab in (0, 1)
        ]
        value, slope = gelu_parts(both[0] + bias_ref[core].astype(F32))
        g_buf[0, q, z] = (both[1] * slope).astype(BF16)
        g_buf[1, q, z] = value.astype(BF16)
        slot = g_buf.at[pl.ds(0, 2), q, z]
        fwd[q, 0] = remote(slot, slot, zp)
        bwd[q, 0] = remote(slot, slot, zm)
        to_sibling(q, 0, z)

    def spread_step(q, s):
        for way, hops, device, i in ((-1, fwd, zp, 0), (1, bwd, zm, 1)):
            owner = (z + NZ + way * s) % NZ
            hops[q, s - 1].wait_recv()
            slot = g_buf.at[pl.ds(i, 1) if s == 3 else pl.ds(0, 2), q, owner]
            hops[q, s] = remote(slot, slot, device)
            to_sibling(q, 2 * s - 1 + i, owner)

    def spread_last(q):
        fwd[q, 3].wait_recv()
        bwd[q, 3].wait_recv()
        to_sibling(q, 7, (z + 4) % NZ)

    def spread_done(q):
        for i in range(8):
            pair[q, i].wait_recv()
        local.append(move(g_buf.at[pl.ds(0, 2), q], g_out.at[:, q, :, :, own_cols]))
        local.append(move(g_buf.at[pl.ds(2, 2), q], g_out.at[:, q, :, :, other_cols]))

    near, far = {}, {}

    def backproject(h):
        grads = [g_buf[half * 2, pl.ds(2 * h, 2)].reshape(256, H) for half in (0, 1)]
        nt = (((1,), (1,)), ((), ()))

        @pl.loop(0, H // TILE)
        def _(n):
            rows = pl.ds(pl.multiple_of(n * TILE, TILE), TILE)
            total = lax.dot_general(grads[0], wx[0, rows], nt, preferred_element_type=F32)
            total += lax.dot_general(grads[1], wu_other[rows], nt, preferred_element_type=F32)
            ig_acc[h, :, :, :, :, rows] = total.reshape(2, 4, 2, R, TILE)

    halves = (pl.ds(0, H // 2), pl.ds(H // 2, H // 2))

    def rows_for(h, side, k):
        if side == 0:
            yk = (y + k) % 4
            return ig_acc[h, yk % 2, :, yk // 2, :, halves[0]]
        return ig_acc[h, :, (x + k) % 4, :, :, halves[1]].reshape(4, R, H // 2)

    def scatter1(h):
        for k in (2, 1, 3):
            for side in (0, 1):
                i = (h * 2 + side) * 3 + k - 1
                s1[i] = enc(rows_for(h, side, k))
                near[h, side, k] = remote(s1.at[i], r1.at[i], (ypeer, xpeer)[side](k))

    def scatter2(h):
        for side in (0, 1):
            total = rows_for(h, side, 0)
            for k in (1, 3, 2):
                near[h, side, k].wait_recv()
                total = total + dec(r1[(h * 2 + side) * 3 + k - 1])
            t1[side] = total
            for k in (2, 1, 3):
                i = (h * 2 + side) * 3 + k - 1
                if side == 0:
                    block = t1[0, (x + k) % 4]
                else:
                    yk = (y + k) % 4
                    block = t1[1, (yk % 2) * 2 + yk // 2]
                s2[i] = enc(block)
                far[h, side, k] = remote(s2.at[i], r2.at[i], (xpeer, ypeer)[side](k))

    def scatter3(h):
        for side in (0, 1):
            total = t1[0, x] if side == 0 else t1[1, par * 2 + yh]
            for k in (1, 3, 2):
                far[h, side, k].wait_recv()
                total = total + dec(r2[(h * 2 + side) * 3 + k - 1])
            ig_out[pl.ds(h * R, R), halves[side]] = total.astype(BF16)

    def transpose(arr):
        for h in (0, 1):
            xt[arr, :, h * 256 : (h + 1) * 256] = x_buf[xi(arr, 0, h)].reshape(256, H).T
        local.append(move(xt.at[arr], xt_out.at[arr]))

    gather1(0)
    w_sib = [
        remote(wu_hbm.at[:, other_cols], wx.at[1], sib),
        remote(wd_hbm.at[:, other_cols], wx.at[3], sib),
    ]
    gather2(0)
    gather1(1)
    gather3(0)
    gather2(1)
    for copy in w_own:
        copy.wait()
    for copy in w_sib:
        copy.wait_recv()
    gathered(0)
    project(0)
    reduce_step(0, 0)
    reduce_step(1, 0)
    reduce_step(0, 1)
    reduce_step(1, 1)
    gather3(1)
    reduce_step(0, 2)
    reduce_step(1, 2)
    gathered(1)
    project(1)
    reduce_step(2, 0)
    reduce_step(3, 0)
    reduce_step(0, 3)
    reduce_step(1, 3)
    reduce_step(2, 1)
    reduce_step(3, 1)
    finish(0)
    finish(1)
    reduce_step(2, 2)
    reduce_step(3, 2)
    spread_step(0, 1)
    spread_step(1, 1)
    reduce_step(2, 3)
    reduce_step(3, 3)
    spread_step(0, 2)
    spread_step(1, 2)
    finish(2)
    finish(3)
    spread_step(0, 3)
    spread_step(1, 3)
    transpose(0)
    spread_step(2, 1)
    spread_step(3, 1)
    spread_last(0)
    spread_last(1)
    transpose(1)
    spread_step(2, 2)
    spread_step(3, 2)
    spread_done(0)
    spread_done(1)
    w_oth.wait()
    backproject(0)
    scatter1(0)
    spread_step(2, 3)
    spread_step(3, 3)
    spread_last(2)
    spread_last(3)
    scatter2(0)
    spread_done(2)
    spread_done(3)
    backproject(1)
    scatter1(1)
    scatter3(0)
    scatter2(1)
    scatter3(1)
    for copy in sent:
        copy.wait_send()
    for copy in local:
        copy.wait()
    assert count["remote"] <= N_SEM and count["local"] <= N_LOCAL


def weight_kernel(g_ref, xt_ref, ig_ref, up_ref, down_ref, bias_ref, ig_out):
    width = g_ref.shape[-1]
    act_grad = g_ref[0].reshape(512, width)
    hidden = g_ref[1].reshape(512, width)
    up_ref[...] = jnp.dot(xt_ref[0], act_grad, preferred_element_type=F32).astype(BF16)
    down_ref[...] = jnp.dot(xt_ref[1], hidden, preferred_element_type=F32).astype(BF16)
    bias_ref[...] = jnp.sum(act_grad.astype(F32), axis=0, keepdims=True)
    ig_out[...] = ig_ref[...]


def body(activations, output_grad, up_weight, down_weight, up_bias):
    anywhere = pl.BlockSpec(memory_space=pl.ANY)
    vmem = pl.BlockSpec(memory_space=pltpu.VMEM)
    g, xt, ig = pl.pallas_call(
        exchange_kernel,
        out_shape=[
            jax.ShapeDtypeStruct((2, 4, NZ, R, 2 * H), BF16),
            jax.ShapeDtypeStruct((2, H, 512), BF16),
            jax.ShapeDtypeStruct((2 * R, H), BF16),
        ],
        in_specs=[anywhere] * 4 + [vmem],
        out_specs=[anywhere, anywhere, vmem],
        scratch_shapes=[
            pltpu.VMEM((8, 2, 4, 2, R, H), BF16),
            pltpu.VMEM((4, H, H), BF16),
            pltpu.VMEM((H, H), BF16),
            pltpu.VMEM((4, 2, NZ, R, H), F32),
            pltpu.VMEM((16, 2, R, H), BF16),
            pltpu.VMEM((16, 2, R, H), BF16),
            pltpu.VMEM((16, 2, R, H), BF16),
            pltpu.VMEM((16, 2, R, H), BF16),
            pltpu.VMEM((4, 4, NZ, R, H), BF16),
            pltpu.VMEM((2, H, 512), BF16),
            pltpu.VMEM((2, 2, 4, 2, R, H), F32),
            pltpu.VMEM((12, 4, R, H // 2), BF16),
            pltpu.VMEM((12, 4, R, H // 2), BF16),
            pltpu.VMEM((2, 4, R, H // 2), F32),
            pltpu.VMEM((12, R, H // 2), BF16),
            pltpu.VMEM((12, R, H // 2), BF16),
            pltpu.SemaphoreType.DMA((N_SEM,)),
            pltpu.SemaphoreType.DMA((N_SEM,)),
            pltpu.SemaphoreType.DMA((N_LOCAL,)),
        ],
        compiler_params=pltpu.CompilerParams(
            collective_id=0, has_side_effects=True, vmem_limit_bytes=56 << 20
        ),
        cost_estimate=pl.CostEstimate(
            flops=3 * 2 * 512 * H * 2 * H, bytes_accessed=12 << 20, transcendentals=64 * H
        ),
        name="exchange",
    )(activations, output_grad, up_weight, down_weight, up_bias.reshape(2, 1, H))
    tile = 256
    up_grad, down_grad, bias_grad, input_grad = pl.pallas_call(
        weight_kernel,
        grid=(2 * H // tile,),
        out_shape=[
            jax.ShapeDtypeStruct((H, 2 * H), BF16),
            jax.ShapeDtypeStruct((H, 2 * H), BF16),
            jax.ShapeDtypeStruct((1, 2 * H), F32),
            jax.ShapeDtypeStruct((2 * R, H), BF16),
        ],
        in_specs=[
            pl.BlockSpec((2, 4, NZ, R, tile), lambda n: (0, 0, 0, 0, n)),
            pl.BlockSpec((2, H, 512), lambda n: (0, 0, 0)),
            pl.BlockSpec((2 * R, H), lambda n: (0, 0)),
        ],
        out_specs=[
            pl.BlockSpec((H, tile), lambda n: (0, n)),
            pl.BlockSpec((H, tile), lambda n: (0, n)),
            pl.BlockSpec((1, tile), lambda n: (0, n)),
            pl.BlockSpec((2 * R, H), lambda n: (0, 0)),
        ],
        compiler_params=pltpu.CompilerParams(vmem_limit_bytes=40 << 20),
        cost_estimate=pl.CostEstimate(
            flops=2 * 2 * 512 * H * 2 * H, bytes_accessed=10 << 20, transcendentals=0
        ),
        name="weight_grads",
    )(g, xt, ig)
    return (input_grad, up_grad, down_grad, bias_grad.reshape(2 * H))


def solution(mesh):
    placed = (P("col", "row"), P("col", "row"), P("row", "col"), P("row", "col"), P("col"))
    return jax.shard_map(
        body,
        mesh=mesh,
        in_specs=placed,
        out_specs=(P("col", "row"), P("row", "col"), P("row", "col"), P("col")),
        check_vma=False,
    )
```

```python
import functools

import jax
import jax.numpy as jnp
from jax import lax
from jax.experimental import pallas as pl
from jax.experimental.pallas import tpu as pltpu
from jax.sharding import PartitionSpec as P

MESH = pl.DeviceIdType.MESH
F32 = jnp.float32
BF16 = jnp.bfloat16

NZ = 8
R = 16
H = 768
TILE = 256

S_GATHER1, S_GATHER2, S_SHARE, S_WEIGHTS, S_CHAIN, S_PAIR, S_NEAR, S_FAR, N_SEND = range(9)
R_GATHER1, R_GATHER2, R_SHARE, R_WEIGHTS, R_CHAIN, R_PAIR, R_NEAR, R_FAR, N_RECV = (
    0, 2, 14, 16, 17, 33, 37, 41, 45,
)
L_IN, L_UP, L_DOWN, L_OTHER, L_BIAS, L_G, L_XT, L_IG, N_LOCAL = 0, 2, 3, 4, 5, 6, 7, 8, 9


def gelu_parts(pre_act):
    coeff = 0.7978845608028654
    cubic = 0.044715
    inner = coeff * (pre_act + cubic * pre_act * pre_act * pre_act)
    tanh_val = jnp.tanh(inner)
    value = 0.5 * pre_act * (1.0 + tanh_val)
    slope = 0.5 * (1.0 + tanh_val) + 0.5 * pre_act * (1.0 - tanh_val * tanh_val) * coeff * (
        1.0 + 3.0 * cubic * pre_act * pre_act
    )
    return (value, slope)


def enc(v):
    return (v * jnp.abs(v)).astype(BF16)


def dec(code):
    v = code.astype(F32)
    root = jnp.sqrt(jnp.abs(v))
    return jnp.where(v < 0, -root, root)


def exchange_kernel(
    act_hbm, og_hbm, wu_hbm, wd_hbm, bias_hbm,
    g_out, xt_out, ig_hbm,
    x_buf, wx, wu_other, part, sp, rp, sm, rm, g_buf, xt, ig_acc,
    s1, r1, t1, s2, r2, bias_buf, ig_out, send_sem, recv_sem, local_sem,
):
    row, col = lax.axis_index("row"), lax.axis_index("col")
    z, core = row // 2, row % 2
    x, y = col // 4, col % 4
    par, yh = y % 2, y // 2

    sib = (z * 2 + 1 - core, col)
    zp = (((z + 1) % NZ) * 2 + core, col)
    zm = (((z + NZ - 1) % NZ) * 2 + core, col)

    def xpeer(k):
        return (row, ((x + k) % 4) * 4 + y)

    def ypeer(k):
        return (row, x * 4 + (y + k) % 4)

    def remote(src, dst, device, sent, received):
        copy = pltpu.make_async_remote_copy(
            src_ref=src, dst_ref=dst, send_sem=send_sem.at[sent], recv_sem=recv_sem.at[received],
            device_id=device, device_id_type=MESH,
        )
        copy.start()
        return copy

    def move(src, dst, i):
        copy = pltpu.make_async_copy(src, dst, local_sem.at[i])
        copy.start()
        return copy

    def wait_for(ref, sem):
        pltpu.make_async_copy(ref, ref, sem).wait()

    own_cols = pl.ds(pl.multiple_of(core * H, H), H)
    other_cols = pl.ds(pl.multiple_of((1 - core) * H, H), H)

    def xi(arr, whose, h):
        return arr * 4 + whose * 2 + h

    for h in range(2):
        for arr, src in ((0, act_hbm), (1, og_hbm)):
            move(src.at[pl.ds(h * R, R)], x_buf.at[xi(arr, 0, h), par, x, yh], L_IN + h)
    weights = [
        move(wu_hbm.at[:, own_cols], wx.at[0], L_UP),
        move(wd_hbm.at[:, own_cols], wx.at[2], L_DOWN),
        move(wu_hbm.at[:, other_cols], wu_other, L_OTHER),
        move(bias_hbm, bias_buf, L_BIAS),
    ]

    barrier = pltpu.get_barrier_semaphore()
    peers = [sib, zp, zm] + [xpeer(k) for k in (1, 2, 3)] + [ypeer(k) for k in (1, 2, 3)]
    for peer in peers:
        pl.semaphore_signal(barrier, inc=1, device_id=peer, device_id_type=MESH)
    pl.semaphore_wait(barrier, len(peers))

    stage2 = {}

    def gather1(h):
        wait_for(x_buf.at[0, 0, 0], local_sem.at[L_IN + h])
        for k in (2, 1, 3):
            for arr, peer in ((0, xpeer(k)), (1, ypeer(k))):
                slot = x_buf.at[xi(arr, 0, h), par, x, yh]
                remote(slot, slot, peer, S_GATHER1, R_GATHER1 + h)

    def group(arr, whose, h, k):
        if arr == 0:
            yk = (y + 4 - k) % 4
            return x_buf.at[xi(0, whose, h), yk % 2, :, yk // 2]
        return x_buf.at[xi(1, whose, h), :, (x + 4 - k) % 4]

    def share(arr, h, k):
        remote(group(arr, 0, h, k), group(arr, 1, h, k), sib, S_SHARE, R_SHARE + h)

    def gather2(h):
        wait_for(x_buf.at[0, 0, pl.ds(0, 3)], recv_sem.at[R_GATHER1 + h])
        for k in (2, 1, 3):
            for arr, peer in ((0, ypeer(k)), (1, xpeer(k))):
                slot = group(arr, 0, h, 0)
                i = R_GATHER2 + (h * 2 + arr) * 3 + k - 1
                stage2[arr, h, k] = remote(slot, slot, peer, S_GATHER2, i)
        for arr in (0, 1):
            share(arr, h, 0)

    def gather3(h):
        for k in (1, 3, 2):
            for arr in (0, 1):
                stage2[arr, h, k].wait_recv()
                share(arr, h, k)

    def gathered(h):
        wait_for(x_buf.at[pl.ds(0, 2)], recv_sem.at[R_SHARE + h])

    def send_weights():
        remote(wu_hbm.at[:, other_cols], wx.at[1], sib, S_WEIGHTS, R_WEIGHTS)
        remote(wd_hbm.at[:, other_cols], wx.at[3], sib, S_WEIGHTS, R_WEIGHTS)

    def own_weights_ready():
        for copy in weights:
            copy.wait()

    def weights_ready():
        wait_for(wx.at[pl.ds(0, 2)], recv_sem.at[R_WEIGHTS])

    def project(h, whose):
        for ab in (0, 1):
            lhs = x_buf[xi(ab, whose, h)].reshape(256, H)

            @pl.loop(0, H // TILE)
            def _(n):
                cols = pl.ds(pl.multiple_of(n * TILE, TILE), TILE)
                total = jnp.dot(lhs, wx[ab * 2 + whose, :, cols], preferred_element_type=F32)
                total = total.reshape(2, NZ, R, TILE)
                if whose == 1:
                    total += part[h * 2 + ab, :, :, :, cols]
                part[h * 2 + ab, :, :, :, cols] = total

    up, down = {}, {}

    def chain_sem(q, way, step):
        return R_CHAIN + q * 4 + way * 2 + step % 2

    def reduce_step(q, s):
        h, p = q // 2, q % 2
        if s > 0:
            up[q, s - 1].wait_recv()
            down[q, s - 1].wait_recv()
        for way, hops, send_buf, recv_buf, device in ((0, up, sp, rp, zp), (1, down, sm, rm, zm)):
            first = way
            owner = (z + 4 - s) % NZ if way == 0 else (z + 4 + s) % NZ
            for ab in (0, 1):
                if s == 0 and ab != first:
                    continue
                v = part[h * 2 + ab, p, owner]
                if s > 1 or (s == 1 and ab == first):
                    v = v + dec(recv_buf[q * 4 + s - 1, ab])
                send_buf[q * 4 + s, ab] = enc(v)
            which = pl.ds(first, 1) if s == 0 else pl.ds(0, 2)
            hops[q, s] = remote(
                send_buf.at[q * 4 + s, which], recv_buf.at[q * 4 + s, which], device,
                S_CHAIN, chain_sem(q, way, s),
            )

    fwd, bwd = {}, {}

    def to_sibling(q, owner):
        remote(
            g_buf.at[pl.ds(0, 2), q, owner], g_buf.at[pl.ds(2, 2), q, owner], sib,
            S_PAIR, R_PAIR + q,
        )

    def finish(q):
        h, p = q // 2, q % 2
        up[q, 3].wait_recv()
        down[q, 3].wait_recv()
        both = [
            part[h * 2 + ab, p, z] + dec(rp[q * 4 + 3, ab]) + dec(rm[q * 4 + 3, ab])
            for ab in (0, 1)
        ]
        bias = bias_buf[...].astype(F32).reshape(1, 2 * H)
        bias = jnp.where(core == 0, bias[:, :H], bias[:, H:])
        value, slope = gelu_parts(both[0] + bias)
        g_buf[0, q, z] = (both[1] * slope).astype(BF16)
        g_buf[1, q, z] = value.astype(BF16)
        slot = g_buf.at[pl.ds(0, 2), q, z]
        fwd[q, 0] = remote(slot, slot, zp, S_CHAIN, chain_sem(q, 0, 0))
        bwd[q, 0] = remote(slot, slot, zm, S_CHAIN, chain_sem(q, 1, 0))
        to_sibling(q, z)

    def spread_step(q, s):
        fwd[q, s - 1].wait_recv()
        bwd[q, s - 1].wait_recv()
        owners = ((z + NZ - s) % NZ, (z + s) % NZ)
        for i, hops, device in ((0, fwd, zp), (1, bwd, zm)):
            slot = g_buf.at[pl.ds(i, 1) if s == 3 else pl.ds(0, 2), q, owners[i]]
            hops[q, s] = remote(slot, slot, device, S_CHAIN, chain_sem(q, i, s))
        for owner in owners:
            to_sibling(q, owner)

    def spread_last(q):
        fwd[q, 3].wait_recv()
        bwd[q, 3].wait_recv()
        to_sibling(q, (z + 4) % NZ)

    def spread_done(q):
        wait_for(g_buf.at[pl.ds(0, 2), q], recv_sem.at[R_PAIR + q])
        move(g_buf.at[pl.ds(0, 2), q], g_out.at[:, q, :, :, own_cols], L_G)
        move(g_buf.at[pl.ds(2, 2), q], g_out.at[:, q, :, :, other_cols], L_G)

    def backproject(h):
        grads = [g_buf[half * 2, pl.ds(2 * h, 2)].reshape(256, H) for half in (0, 1)]
        nt = (((1,), (1,)), ((), ()))

        @pl.loop(0, H // TILE)
        def _(n):
            rows = pl.ds(pl.multiple_of(n * TILE, TILE), TILE)
            total = lax.dot_general(grads[0], wx[0, rows], nt, preferred_element_type=F32)
            total += lax.dot_general(grads[1], wu_other[rows], nt, preferred_element_type=F32)
            ig_acc[h, :, :, :, :, rows] = total.reshape(2, 4, 2, R, TILE)

    halves = (pl.ds(0, H // 2), pl.ds(H // 2, H // 2))

    def rows_for(h, side, k):
        if side == 0:
            yk = (y + k) % 4
            return ig_acc[h, yk % 2, :, yk // 2, :, halves[0]]
        return ig_acc[h, :, (x + k) % 4, :, :, halves[1]].reshape(4, R, H // 2)

    def scatter1(h):
        for k in (2, 1, 3):
            for side in (0, 1):
                i = (h * 2 + side) * 3 + k - 1
                s1[i] = enc(rows_for(h, side, k))
                remote(
                    s1.at[i], r1.at[i], (ypeer, xpeer)[side](k), S_NEAR, R_NEAR + h * 2 + side
                )

    def scatter2(h):
        for side in (0, 1):
            total = rows_for(h, side, 0)
            wait_for(r1.at[pl.ds(0, 3)], recv_sem.at[R_NEAR + h * 2 + side])
            for k in (1, 3, 2):
                total = total + dec(r1[(h * 2 + side) * 3 + k - 1])
            t1[side] = total
            for k in (2, 1, 3):
                i = (h * 2 + side) * 3 + k - 1
                if side == 0:
                    block = t1[0, (x + k) % 4]
                else:
                    yk = (y + k) % 4
                    block = t1[1, (yk % 2) * 2 + yk // 2]
                s2[i] = enc(block)
                remote(
                    s2.at[i], r2.at[i], (xpeer, ypeer)[side](k), S_FAR, R_FAR + h * 2 + side
                )

    def scatter3(h):
        for side in (0, 1):
            total = t1[0, x] if side == 0 else t1[1, par * 2 + yh]
            wait_for(r2.at[pl.ds(0, 3)], recv_sem.at[R_FAR + h * 2 + side])
            for k in (1, 3, 2):
                total = total + dec(r2[(h * 2 + side) * 3 + k - 1])
            ig_out[pl.ds(h * R, R), halves[side]] = total.astype(BF16)
        move(ig_out.at[pl.ds(h * R, R)], ig_hbm.at[pl.ds(h * R, R)], L_IG)

    def transpose(arr):
        for h in (0, 1):
            xt[arr, :, h * 256 : (h + 1) * 256] = x_buf[xi(arr, 0, h)].reshape(256, H).T
        move(xt.at[arr], xt_out.at[arr], L_XT)

    def drain():
        for ref, i in (
            (x_buf.at[0, :, pl.ds(0, 3)], S_GATHER1),
            (x_buf.at[pl.ds(0, 3)], S_GATHER2),
            (x_buf.at[pl.ds(0, 4)], S_SHARE),
            (wx.at[pl.ds(0, 2)], S_WEIGHTS),
            (g_buf.at[:, :, pl.ds(0, 7)], S_CHAIN),
            (g_buf.at[pl.ds(0, 2)], S_PAIR),
            (s1, S_NEAR),
            (s2, S_FAR),
        ):
            wait_for(ref, send_sem.at[i])
        for ref, i in ((g_buf, L_G), (xt, L_XT), (ig_out, L_IG)):
            wait_for(ref, local_sem.at[i])

    gather1(0)
    send_weights()
    gather2(0)
    gather1(1)
    gather3(0)
    gather2(1)
    own_weights_ready()
    project(0, 0)
    weights_ready()
    gathered(0)
    project(0, 1)
    reduce_step(0, 0)
    reduce_step(1, 0)
    reduce_step(0, 1)
    reduce_step(1, 1)
    gather3(1)
    project(1, 0)
    reduce_step(0, 2)
    reduce_step(1, 2)
    gathered(1)
    project(1, 1)
    reduce_step(2, 0)
    reduce_step(3, 0)
    reduce_step(0, 3)
    reduce_step(1, 3)
    reduce_step(2, 1)
    reduce_step(3, 1)
    finish(0)
    finish(1)
    reduce_step(2, 2)
    reduce_step(3, 2)
    spread_step(0, 1)
    spread_step(1, 1)
    reduce_step(2, 3)
    reduce_step(3, 3)
    spread_step(0, 2)
    spread_step(1, 2)
    finish(2)
    finish(3)
    spread_step(0, 3)
    spread_step(1, 3)
    transpose(0)
    spread_step(2, 1)
    spread_step(3, 1)
    spread_last(0)
    spread_last(1)
    transpose(1)
    spread_step(2, 2)
    spread_step(3, 2)
    spread_done(0)
    spread_done(1)
    backproject(0)
    scatter1(0)
    spread_step(2, 3)
    spread_step(3, 3)
    spread_last(2)
    spread_last(3)
    scatter2(0)
    spread_done(2)
    spread_done(3)
    backproject(1)
    scatter1(1)
    scatter3(0)
    scatter2(1)
    scatter3(1)
    drain()


def weight_kernel(g_ref, xt_ref, ig_ref, up_ref, down_ref, bias_ref, ig_out):
    width = g_ref.shape[-1]
    act_grad = g_ref[0].reshape(512, width)
    hidden = g_ref[1].reshape(512, width)
    up_ref[...] = jnp.dot(xt_ref[0], act_grad, preferred_element_type=F32).astype(BF16)
    down_ref[...] = jnp.dot(xt_ref[1], hidden, preferred_element_type=F32).astype(BF16)
    start = pl.multiple_of(pl.program_id(0) * width, width)
    bias_ref[pl.ds(start, width)] = jnp.sum(act_grad.astype(F32), axis=0)
    ig_out[...] = ig_ref[...]


def body(activations, output_grad, up_weight, down_weight, up_bias):
    anywhere = pl.BlockSpec(memory_space=pl.ANY)
    g, xt, ig = pl.pallas_call(
        exchange_kernel,
        out_shape=[
            jax.ShapeDtypeStruct((2, 4, NZ, R, 2 * H), BF16),
            jax.ShapeDtypeStruct((2, H, 512), BF16),
            jax.ShapeDtypeStruct((2 * R, H), BF16),
        ],
        in_specs=[anywhere] * 5,
        out_specs=[anywhere] * 3,
        scratch_shapes=[
            pltpu.VMEM((8, 2, 4, 2, R, H), BF16),
            pltpu.VMEM((4, H, H), BF16),
            pltpu.VMEM((H, H), BF16),
            pltpu.VMEM((4, 2, NZ, R, H), F32),
            pltpu.VMEM((16, 2, R, H), BF16),
            pltpu.VMEM((16, 2, R, H), BF16),
            pltpu.VMEM((16, 2, R, H), BF16),
            pltpu.VMEM((16, 2, R, H), BF16),
            pltpu.VMEM((4, 4, NZ, R, H), BF16),
            pltpu.VMEM((2, H, 512), BF16),
            pltpu.VMEM((2, 2, 4, 2, R, H), F32),
            pltpu.VMEM((12, 4, R, H // 2), BF16),
            pltpu.VMEM((12, 4, R, H // 2), BF16),
            pltpu.VMEM((2, 4, R, H // 2), F32),
            pltpu.VMEM((12, R, H // 2), BF16),
            pltpu.VMEM((12, R, H // 2), BF16),
            pltpu.VMEM((2 * H,), BF16),
            pltpu.VMEM((2 * R, H), BF16),
            pltpu.SemaphoreType.DMA((N_SEND,)),
            pltpu.SemaphoreType.DMA((N_RECV,)),
            pltpu.SemaphoreType.DMA((N_LOCAL,)),
        ],
        compiler_params=pltpu.CompilerParams(
            collective_id=0, has_side_effects=True, vmem_limit_bytes=56 << 20
        ),
        cost_estimate=pl.CostEstimate(
            flops=3 * 2 * 512 * H * 2 * H, bytes_accessed=12 << 20, transcendentals=64 * H
        ),
        name="exchange",
    )(activations, output_grad, up_weight, down_weight, up_bias)
    tile = 256
    up_grad, down_grad, bias_grad, input_grad = pl.pallas_call(
        weight_kernel,
        grid=(2 * H // tile,),
        out_shape=[
            jax.ShapeDtypeStruct((H, 2 * H), BF16),
            jax.ShapeDtypeStruct((H, 2 * H), BF16),
            jax.ShapeDtypeStruct((2 * H,), F32),
            jax.ShapeDtypeStruct((2 * R, H), BF16),
        ],
        in_specs=[
            pl.BlockSpec((2, 4, NZ, R, tile), lambda n: (0, 0, 0, 0, n)),
            pl.BlockSpec((2, H, 512), lambda n: (0, 0, 0)),
            pl.BlockSpec((2 * R, H), lambda n: (0, 0)),
        ],
        out_specs=[
            pl.BlockSpec((H, tile), lambda n: (0, n)),
            pl.BlockSpec((H, tile), lambda n: (0, n)),
            pl.BlockSpec((2 * H,), lambda n: (0,)),
            pl.BlockSpec((2 * R, H), lambda n: (0, 0)),
        ],
        compiler_params=pltpu.CompilerParams(vmem_limit_bytes=60 << 20),
        cost_estimate=pl.CostEstimate(
            flops=2 * 2 * 512 * H * 2 * H, bytes_accessed=10 << 20, transcendentals=0
        ),
        name="weight_grads",
    )(g, xt, ig)
    return (input_grad, up_grad, down_grad, bias_grad)


def solution(mesh):
    placed = (P("col", "row"), P("col", "row"), P("row", "col"), P("row", "col"), P("col"))
    return jax.shard_map(
        body,
        mesh=mesh,
        in_specs=placed,
        out_specs=(P("col", "row"), P("row", "col"), P("row", "col"), P("col")),
        check_vma=False,
    )
```

```python
import functools

import jax
import jax.numpy as jnp
from jax import lax
from jax.experimental import pallas as pl
from jax.experimental.pallas import tpu as pltpu
from jax.sharding import PartitionSpec as P

MESH = pl.DeviceIdType.MESH
F32 = jnp.float32
BF16 = jnp.bfloat16

NZ = 8
R = 16
H = 768
HALF = H // 2

S_GATHER1, S_GATHER2, S_SHARE, S_WEIGHTS, S_CHAIN, S_PAIR, S_NEAR, S_FAR, N_SEND = range(9)
R_GATHER1, R_GATHER2, R_SHARE, R_WEIGHTS, R_CHAIN, R_PAIR, R_NEAR, R_FAR, N_RECV = (
    0, 2, 14, 16, 17, 49, 53, 57, 61,
)
L_IN, L_UP, L_DOWN, L_OTHER, L_BIAS, N_LOCAL = 0, 2, 3, 4, 5, 6


def gelu_parts(pre_act):
    coeff = 0.7978845608028654
    cubic = 0.044715
    inner = coeff * (pre_act + cubic * pre_act * pre_act * pre_act)
    tanh_val = jnp.tanh(inner)
    value = 0.5 * pre_act * (1.0 + tanh_val)
    slope = 0.5 * (1.0 + tanh_val) + 0.5 * pre_act * (1.0 - tanh_val * tanh_val) * coeff * (
        1.0 + 3.0 * cubic * pre_act * pre_act
    )
    return (value, slope)


def enc(v):
    return (v * jnp.abs(v)).astype(BF16)


def dec(code):
    v = code.astype(F32)
    root = jnp.sqrt(jnp.abs(v))
    return jnp.where(v < 0, -root, root)


def exchange_kernel(
    act_hbm, og_hbm, wu_hbm, wd_hbm, bias_hbm,
    up_out, down_out, bias_out, ig_out,
    x_buf, wx, wu_other, part, sp, rp, sm, rm, g_buf, ig_acc,
    s1, r1, t1, s2, r2, bias_buf, send_sem, recv_sem, local_sem,
):
    row, col = lax.axis_index("row"), lax.axis_index("col")
    z, core = row // 2, row % 2
    x, y = col // 4, col % 4
    par, yh = y % 2, y // 2

    sib = (z * 2 + 1 - core, col)
    zp = (((z + 1) % NZ) * 2 + core, col)
    zm = (((z + NZ - 1) % NZ) * 2 + core, col)

    def xpeer(k):
        return (row, ((x + k) % 4) * 4 + y)

    def ypeer(k):
        return (row, x * 4 + (y + k) % 4)

    def remote(src, dst, device, sent, received):
        copy = pltpu.make_async_remote_copy(
            src_ref=src, dst_ref=dst, send_sem=send_sem.at[sent], recv_sem=recv_sem.at[received],
            device_id=device, device_id_type=MESH,
        )
        copy.start()
        return copy

    def move(src, dst, i):
        copy = pltpu.make_async_copy(src, dst, local_sem.at[i])
        copy.start()
        return copy

    def wait_for(ref, sem):
        pltpu.make_async_copy(ref, ref, sem).wait()

    own_cols = pl.ds(pl.multiple_of(core * H, H), H)
    other_cols = pl.ds(pl.multiple_of((1 - core) * H, H), H)

    def xi(arr, whose, h):
        return arr * 4 + whose * 2 + h

    for h in range(2):
        for arr, src in ((0, act_hbm), (1, og_hbm)):
            move(src.at[pl.ds(h * R, R)], x_buf.at[xi(arr, 0, h), par, x, yh], L_IN + h)
    weights = [
        move(wu_hbm.at[:, own_cols], wx.at[0], L_UP),
        move(wd_hbm.at[:, own_cols], wx.at[2], L_DOWN),
        move(wu_hbm.at[:, other_cols], wu_other, L_OTHER),
        move(bias_hbm, bias_buf, L_BIAS),
    ]

    barrier = pltpu.get_barrier_semaphore()
    peers = [sib, zp, zm] + [xpeer(k) for k in (1, 2, 3)] + [ypeer(k) for k in (1, 2, 3)]
    for peer in peers:
        pl.semaphore_signal(barrier, inc=1, device_id=peer, device_id_type=MESH)
    pl.semaphore_wait(barrier, len(peers))

    stage2 = {}

    def gather1(h):
        wait_for(x_buf.at[0, 0, 0], local_sem.at[L_IN + h])
        for k in (2, 1, 3):
            for arr, peer in ((0, xpeer(k)), (1, ypeer(k))):
                slot = x_buf.at[xi(arr, 0, h), par, x, yh]
                remote(slot, slot, peer, S_GATHER1, R_GATHER1 + h)

    def group(arr, whose, h, k):
        if arr == 0:
            yk = (y + 4 - k) % 4
            return x_buf.at[xi(0, whose, h), yk % 2, :, yk // 2]
        return x_buf.at[xi(1, whose, h), :, (x + 4 - k) % 4]

    def share(arr, h, k):
        remote(group(arr, 0, h, k), group(arr, 1, h, k), sib, S_SHARE, R_SHARE + h)

    def gather2(h):
        wait_for(x_buf.at[0, 0, pl.ds(0, 3)], recv_sem.at[R_GATHER1 + h])
        for k in (2, 1, 3):
            for arr, peer in ((0, ypeer(k)), (1, xpeer(k))):
                slot = group(arr, 0, h, 0)
                i = R_GATHER2 + (h * 2 + arr) * 3 + k - 1
                stage2[arr, h, k] = remote(slot, slot, peer, S_GATHER2, i)
        for arr in (0, 1):
            share(arr, h, 0)

    def gather3(h, *hops):
        for k in hops:
            for arr in (0, 1):
                stage2[arr, h, k].wait_recv()
                share(arr, h, k)

    def gathered(h):
        wait_for(x_buf.at[pl.ds(0, 2)], recv_sem.at[R_SHARE + h])

    def send_weights():
        remote(wu_hbm.at[:, other_cols], wx.at[1], sib, S_WEIGHTS, R_WEIGHTS)
        remote(wd_hbm.at[:, other_cols], wx.at[3], sib, S_WEIGHTS, R_WEIGHTS)

    def own_weights_ready():
        for copy in weights:
            copy.wait()

    def weights_ready():
        wait_for(wx.at[pl.ds(0, 2)], recv_sem.at[R_WEIGHTS])

    def project(h, whose):
        for ab in (0, 1):
            lhs = x_buf[xi(ab, whose, h)].reshape(256, H)

            total = jnp.dot(lhs, wx[ab * 2 + whose], preferred_element_type=F32)
            total = total.reshape(2, NZ, R, H)
            if whose == 1:
                total += part[h * 2 + ab]
            part[h * 2 + ab] = total

    up, down = {}, {}

    def chunk(q):
        return q // 4, q // 2 % 2, pl.ds(q % 2 * HALF, HALF)

    def chain_sem(q, way, step):
        return R_CHAIN + q * 4 + way * 2 + step % 2

    def reduce_step(q, s):
        h, p, c = chunk(q)
        if s > 0:
            up[q, s - 1].wait_recv()
            down[q, s - 1].wait_recv()
        for way, hops, send_buf, recv_buf, device in ((0, up, sp, rp, zp), (1, down, sm, rm, zm)):
            first = way
            owner = (z + 4 - s) % NZ if way == 0 else (z + 4 + s) % NZ
            for ab in (0, 1):
                if s == 0 and ab != first:
                    continue
                v = part[h * 2 + ab, p, owner, :, c]
                if s > 1 or (s == 1 and ab == first):
                    v = v + dec(recv_buf[q * 4 + s - 1, ab])
                send_buf[q * 4 + s, ab] = enc(v)
            which = pl.ds(first, 1) if s == 0 else pl.ds(0, 2)
            hops[q, s] = remote(
                send_buf.at[q * 4 + s, which], recv_buf.at[q * 4 + s, which], device,
                S_CHAIN, chain_sem(q, way, s),
            )

    fwd, bwd = {}, {}

    def to_sibling(q, owner):
        if q % 2 == 1:
            t = q // 2
            remote(
                g_buf.at[pl.ds(0, 2), t, owner], g_buf.at[pl.ds(2, 2), t, owner], sib,
                S_PAIR, R_PAIR + t,
            )

    def finish(q):
        h, p, c = chunk(q)
        up[q, 3].wait_recv()
        down[q, 3].wait_recv()
        both = [
            part[h * 2 + ab, p, z, :, c] + dec(rp[q * 4 + 3, ab]) + dec(rm[q * 4 + 3, ab])
            for ab in (0, 1)
        ]
        bias = bias_buf[...].astype(F32).reshape(1, 2 * H)
        bias = jnp.where(core == 0, bias[:, :H], bias[:, H:])[:, q % 2 * HALF : (q % 2 + 1) * HALF]
        value, slope = gelu_parts(both[0] + bias)
        g_buf[0, q // 2, z, :, c] = (both[1] * slope).astype(BF16)
        g_buf[1, q // 2, z, :, c] = value.astype(BF16)
        slot = g_buf.at[pl.ds(0, 2), q // 2, z, :, c]
        fwd[q, 0] = remote(slot, slot, zp, S_CHAIN, chain_sem(q, 0, 0))
        bwd[q, 0] = remote(slot, slot, zm, S_CHAIN, chain_sem(q, 1, 0))
        to_sibling(q, z)

    def spread_step(q, s):
        c = chunk(q)[2]
        fwd[q, s - 1].wait_recv()
        bwd[q, s - 1].wait_recv()
        owners = ((z + NZ - s) % NZ, (z + s) % NZ)
        for i, hops, device in ((0, fwd, zp), (1, bwd, zm)):
            which = pl.ds(i, 1) if s == 3 else pl.ds(0, 2)
            slot = g_buf.at[which, q // 2, owners[i], :, c]
            hops[q, s] = remote(slot, slot, device, S_CHAIN, chain_sem(q, i, s))
        for owner in owners:
            to_sibling(q, owner)

    def spread_last(q):
        fwd[q, 3].wait_recv()
        bwd[q, 3].wait_recv()
        to_sibling(q, (z + 4) % NZ)

    def spread_done(t):
        wait_for(g_buf.at[pl.ds(0, 2), t], recv_sem.at[R_PAIR + t])

    def backproject(h):
        grads = [g_buf[half * 2, pl.ds(2 * h, 2)].reshape(256, H) for half in (0, 1)]
        nt = (((1,), (1,)), ((), ()))

        total = lax.dot_general(grads[0], wx[0], nt, preferred_element_type=F32)
        total += lax.dot_general(grads[1], wu_other[...], nt, preferred_element_type=F32)
        ig_acc[h] = total.reshape(2, 4, 2, R, H)

    halves = (pl.ds(0, HALF), pl.ds(HALF, HALF))

    def rows_for(h, side, k):
        if side == 0:
            yk = (y + k) % 4
            return ig_acc[h, yk % 2, :, yk // 2, :, halves[0]]
        return ig_acc[h, :, (x + k) % 4, :, :, halves[1]].reshape(4, R, HALF)

    def scatter1(h):
        for k in (2, 1, 3):
            for side in (0, 1):
                i = (h * 2 + side) * 3 + k - 1
                s1[i] = enc(rows_for(h, side, k))
                remote(
                    s1.at[i], r1.at[i], (ypeer, xpeer)[side](k), S_NEAR, R_NEAR + h * 2 + side
                )

    def scatter2(h):
        for side in (0, 1):
            total = rows_for(h, side, 0)
            wait_for(r1.at[pl.ds(0, 3)], recv_sem.at[R_NEAR + h * 2 + side])
            for k in (1, 3, 2):
                total = total + dec(r1[(h * 2 + side) * 3 + k - 1])
            t1[side] = total
            for k in (2, 1, 3):
                i = (h * 2 + side) * 3 + k - 1
                if side == 0:
                    block = t1[0, (x + k) % 4]
                else:
                    yk = (y + k) % 4
                    block = t1[1, (yk % 2) * 2 + yk // 2]
                s2[i] = enc(block)
                remote(
                    s2.at[i], r2.at[i], (xpeer, ypeer)[side](k), S_FAR, R_FAR + h * 2 + side
                )

    def scatter3(h):
        for side in (0, 1):
            total = t1[0, x] if side == 0 else t1[1, par * 2 + yh]
            wait_for(r2.at[pl.ds(0, 3)], recv_sem.at[R_FAR + h * 2 + side])
            for k in (1, 3, 2):
                total = total + dec(r2[(h * 2 + side) * 3 + k - 1])
            ig_out[pl.ds(h * R, R), halves[side]] = total.astype(BF16)

    def weight_grad(arr, half):
        tokens = x_buf[pl.ds(xi(arr, 0, 0), 2)].reshape(512, H)
        grads = g_buf[half * 2 + arr].reshape(512, H)
        tn = (((0,), (0,)), ((), ()))
        total = lax.dot_general(tokens, grads, tn, preferred_element_type=F32)
        (up_out, down_out)[arr][half] = total.astype(BF16)

    def bias_grad():
        own, other = [
            jnp.sum(g_buf[i].reshape(512, H).astype(F32), axis=0, keepdims=True) for i in (0, 2)
        ]
        left, right = jnp.where(core == 0, own, other), jnp.where(core == 0, other, own)
        bias_out[...] = jnp.concatenate([left, right], axis=1).reshape(2 * H)

    def drain():
        for ref, i in (
            (x_buf.at[0, :, pl.ds(0, 3)], S_GATHER1),
            (x_buf.at[pl.ds(0, 3)], S_GATHER2),
            (x_buf.at[pl.ds(0, 4)], S_SHARE),
            (wx.at[pl.ds(0, 2)], S_WEIGHTS),
            (g_buf.at[:, :, pl.ds(0, 7)], S_CHAIN),
            (g_buf.at[pl.ds(0, 2)], S_PAIR),
            (s1, S_NEAR),
            (s2, S_FAR),
        ):
            wait_for(ref, send_sem.at[i])

    gather1(0)
    gather1(1)
    send_weights()
    gather2(0)
    gather3(0, 1)
    gather2(1)
    gather3(0, 3, 2)
    own_weights_ready()
    project(0, 0)
    weights_ready()
    gathered(0)
    project(0, 1)
    for q in range(4):
        reduce_step(q, 0)
    gather3(1, 1, 3, 2)
    for q in range(4):
        reduce_step(q, 1)
    project(1, 0)
    gathered(1)
    project(1, 1)
    for q in range(4):
        reduce_step(4 + q, 0)
    for q in range(4):
        reduce_step(q, 2)
    for q in range(4):
        reduce_step(4 + q, 1)
    for q in range(4):
        reduce_step(q, 3)
    for q in range(4):
        reduce_step(4 + q, 2)
    for q in range(4):
        finish(q)
    for q in range(4):
        reduce_step(4 + q, 3)
    for q in range(4):
        spread_step(q, 1)
    for q in range(4):
        finish(4 + q)
    for q in range(4):
        spread_step(q, 2)
    for q in range(4):
        spread_step(4 + q, 1)
    for q in range(4):
        spread_step(q, 3)
    for q in range(4):
        spread_step(4 + q, 2)
    for q in range(4):
        spread_last(q)
    for q in range(4):
        spread_step(4 + q, 3)
    spread_done(0)
    spread_done(1)
    backproject(0)
    scatter1(0)
    for q in range(4):
        spread_last(4 + q)
    scatter2(0)
    spread_done(2)
    spread_done(3)
    backproject(1)
    scatter1(1)
    scatter3(0)
    weight_grad(0, 0)
    weight_grad(0, 1)
    scatter2(1)
    weight_grad(1, 0)
    weight_grad(1, 1)
    bias_grad()
    scatter3(1)
    drain()


def place_kernel(up_ref, down_ref, bias_ref, ig_ref, up_hbm, down_hbm, bias_hbm, ig_hbm, sem):
    core = lax.axis_index("row") % 2
    copies = [
        pltpu.make_async_copy(bias_ref, bias_hbm, sem.at[4]),
        pltpu.make_async_copy(ig_ref, ig_hbm, sem.at[5]),
    ]
    for half in (0, 1):
        start = pl.multiple_of((core if half == 0 else 1 - core) * H, H)
        for arr, src, dst in ((0, up_ref, up_hbm), (1, down_ref, down_hbm)):
            cols = dst.at[:, pl.ds(start, H)]
            copies.append(pltpu.make_async_copy(src.at[half], cols, sem.at[half * 2 + arr]))
    for copy in copies:
        copy.start()
    for copy in copies:
        copy.wait()


def body(activations, output_grad, up_weight, down_weight, up_bias):
    anywhere = pl.BlockSpec(memory_space=pl.ANY)
    hbm = pl.BlockSpec(memory_space=pltpu.HBM)
    vmem = pl.BlockSpec(memory_space=pltpu.VMEM)
    operands = [
        pltpu.with_memory_space_constraint(a, pltpu.HBM)
        for a in (activations, output_grad, up_weight, down_weight, up_bias)
    ]
    results = pl.pallas_call(
        exchange_kernel,
        out_shape=[
            pltpu.VMEM((2, H, H), BF16),
            pltpu.VMEM((2, H, H), BF16),
            pltpu.VMEM((2 * H,), F32),
            pltpu.VMEM((2 * R, H), BF16),
        ],
        in_specs=[hbm] * 5,
        out_specs=[vmem] * 4,
        scratch_shapes=[
            pltpu.VMEM((8, 2, 4, 2, R, H), BF16),
            pltpu.VMEM((4, H, H), BF16),
            pltpu.VMEM((H, H), BF16),
            pltpu.VMEM((4, 2, NZ, R, H), F32),
            pltpu.VMEM((32, 2, R, HALF), BF16),
            pltpu.VMEM((32, 2, R, HALF), BF16),
            pltpu.VMEM((32, 2, R, HALF), BF16),
            pltpu.VMEM((32, 2, R, HALF), BF16),
            pltpu.VMEM((4, 4, NZ, R, H), BF16),
            pltpu.VMEM((2, 2, 4, 2, R, H), F32),
            pltpu.VMEM((12, 4, R, HALF), BF16),
            pltpu.VMEM((12, 4, R, HALF), BF16),
            pltpu.VMEM((2, 4, R, HALF), F32),
            pltpu.VMEM((12, R, HALF), BF16),
            pltpu.VMEM((12, R, HALF), BF16),
            pltpu.VMEM((2 * H,), BF16),
            pltpu.SemaphoreType.DMA((N_SEND,)),
            pltpu.SemaphoreType.DMA((N_RECV,)),
            pltpu.SemaphoreType.DMA((N_LOCAL,)),
        ],
        compiler_params=pltpu.CompilerParams(
            collective_id=0, has_side_effects=True, vmem_limit_bytes=44 << 20
        ),
        cost_estimate=pl.CostEstimate(
            flops=5 * 2 * 512 * H * 2 * H, bytes_accessed=12 << 20, transcendentals=64 * H
        ),
        name="exchange",
    )(*operands)
    up_grad, down_grad, bias_grad, input_grad = pl.pallas_call(
        place_kernel,
        out_shape=[
            jax.ShapeDtypeStruct((H, 2 * H), BF16),
            jax.ShapeDtypeStruct((H, 2 * H), BF16),
            jax.ShapeDtypeStruct((2 * H,), F32),
            jax.ShapeDtypeStruct((2 * R, H), BF16),
        ],
        in_specs=[anywhere] * 4,
        out_specs=[hbm] * 4,
        scratch_shapes=[pltpu.SemaphoreType.DMA((6,))],
        compiler_params=pltpu.CompilerParams(vmem_limit_bytes=1 << 20),
        cost_estimate=pl.CostEstimate(flops=0, bytes_accessed=5 << 20, transcendentals=0),
        name="place",
    )(*results)
    return (input_grad, up_grad, down_grad, bias_grad)


def solution(mesh):
    placed = (P("col", "row"), P("col", "row"), P("row", "col"), P("row", "col"), P("col"))
    return jax.shard_map(
        body,
        mesh=mesh,
        in_specs=placed,
        out_specs=(P("col", "row"), P("row", "col"), P("row", "col"), P("col")),
        check_vma=False,
    )
```

```python
import functools

import jax
import jax.numpy as jnp
from jax import lax
from jax.experimental import pallas as pl
from jax.experimental.pallas import tpu as pltpu
from jax.sharding import PartitionSpec as P

MESH = pl.DeviceIdType.MESH
F32 = jnp.float32
BF16 = jnp.bfloat16

NZ = 8
R = 16
H = 768
HALF = H // 2

S_GATHER1, S_GATHER2, S_SHARE, S_WEIGHTS, S_CHAIN, S_PAIR, S_NEAR, S_FAR, N_SEND = range(9)
R_GATHER1, R_GATHER2, R_SHARE, R_WEIGHTS, R_CHAIN, R_PAIR, R_NEAR, R_FAR, N_RECV = (
    0, 2, 14, 16, 17, 49, 53, 57, 61,
)
L_IN, L_UP, L_DOWN, L_OTHER, L_BIAS, N_LOCAL = 0, 2, 3, 4, 5, 6


def gelu_parts(pre_act):
    coeff = 0.7978845608028654
    cubic = 0.044715
    inner = coeff * (pre_act + cubic * pre_act * pre_act * pre_act)
    tanh_val = jnp.tanh(inner)
    value = 0.5 * pre_act * (1.0 + tanh_val)
    slope = 0.5 * (1.0 + tanh_val) + 0.5 * pre_act * (1.0 - tanh_val * tanh_val) * coeff * (
        1.0 + 3.0 * cubic * pre_act * pre_act
    )
    return (value, slope)


def enc(v):
    return (v * jnp.abs(v)).astype(BF16)


def dec(code):
    v = code.astype(F32)
    root = jnp.sqrt(jnp.abs(v))
    return jnp.where(v < 0, -root, root)


def exchange_kernel(
    act_hbm, og_hbm, wu_hbm, wd_hbm, bias_hbm,
    up_out, down_out, bias_out, ig_out,
    x_buf, wx, wu_other, part, sp, rp, sm, rm, g_buf, ig_acc,
    s1, r1, t1, s2, r2, bias_buf, send_sem, recv_sem, local_sem,
):
    row, col = lax.axis_index("row"), lax.axis_index("col")
    z, core = row // 2, row % 2
    x, y = col // 4, col % 4
    par, yh = y % 2, y // 2

    sib = (z * 2 + 1 - core, col)
    zp = (((z + 1) % NZ) * 2 + core, col)
    zm = (((z + NZ - 1) % NZ) * 2 + core, col)

    def xpeer(k):
        return (row, ((x + k) % 4) * 4 + y)

    def ypeer(k):
        return (row, x * 4 + (y + k) % 4)

    def remote(src, dst, device, sent, received):
        copy = pltpu.make_async_remote_copy(
            src_ref=src, dst_ref=dst, send_sem=send_sem.at[sent], recv_sem=recv_sem.at[received],
            device_id=device, device_id_type=MESH,
        )
        copy.start()
        return copy

    def move(src, dst, i):
        copy = pltpu.make_async_copy(src, dst, local_sem.at[i])
        copy.start()
        return copy

    def wait_for(ref, sem):
        pltpu.make_async_copy(ref, ref, sem).wait()

    own_cols = pl.ds(pl.multiple_of(core * H, H), H)
    other_cols = pl.ds(pl.multiple_of((1 - core) * H, H), H)

    def xi(arr, whose, h):
        return arr * 4 + whose * 2 + h

    for h in range(2):
        for arr, src in ((0, act_hbm), (1, og_hbm)):
            move(src.at[pl.ds(h * R, R)], x_buf.at[xi(arr, 0, h), par, x, yh], L_IN + h)
    weights = [
        move(wu_hbm.at[:, own_cols], wx.at[0], L_UP),
        move(wd_hbm.at[:, own_cols], wx.at[2], L_DOWN),
        move(wu_hbm.at[:, other_cols], wu_other, L_OTHER),
        move(bias_hbm, bias_buf, L_BIAS),
    ]

    barrier = pltpu.get_barrier_semaphore()
    peers = [sib, zp, zm] + [xpeer(k) for k in (1, 2, 3)] + [ypeer(k) for k in (1, 2, 3)]
    for peer in peers:
        pl.semaphore_signal(barrier, inc=1, device_id=peer, device_id_type=MESH)
    pl.semaphore_wait(barrier, len(peers))

    stage2 = {}

    def gather1(h):
        wait_for(x_buf.at[0, 0, 0], local_sem.at[L_IN + h])
        for k in (2, 1, 3):
            for arr, peer in ((0, xpeer(k)), (1, ypeer(k))):
                slot = x_buf.at[xi(arr, 0, h), par, x, yh]
                remote(slot, slot, peer, S_GATHER1, R_GATHER1 + h)

    def group(arr, whose, h, k):
        if arr == 0:
            yk = (y + 4 - k) % 4
            return x_buf.at[xi(0, whose, h), yk % 2, :, yk // 2]
        return x_buf.at[xi(1, whose, h), :, (x + 4 - k) % 4]

    def share(arr, h, k):
        remote(group(arr, 0, h, k), group(arr, 1, h, k), sib, S_SHARE, R_SHARE + h)

    def gather2(h):
        wait_for(x_buf.at[0, 0, pl.ds(0, 3)], recv_sem.at[R_GATHER1 + h])
        for k in (2, 1, 3):
            for arr, peer in ((0, ypeer(k)), (1, xpeer(k))):
                slot = group(arr, 0, h, 0)
                i = R_GATHER2 + (h * 2 + arr) * 3 + k - 1
                stage2[arr, h, k] = remote(slot, slot, peer, S_GATHER2, i)
        for arr in (0, 1):
            share(arr, h, 0)

    def gather3(h, *hops):
        for k in hops:
            for arr in (0, 1):
                stage2[arr, h, k].wait_recv()
                share(arr, h, k)

    def gathered(h):
        wait_for(x_buf.at[pl.ds(0, 2)], recv_sem.at[R_SHARE + h])

    def send_weights():
        remote(wu_hbm.at[:, other_cols], wx.at[1], sib, S_WEIGHTS, R_WEIGHTS)
        remote(wd_hbm.at[:, other_cols], wx.at[3], sib, S_WEIGHTS, R_WEIGHTS)

    def own_weights_ready():
        for copy in weights:
            copy.wait()

    def weights_ready():
        wait_for(wx.at[pl.ds(0, 2)], recv_sem.at[R_WEIGHTS])

    def project(h, whose):
        for ab in (0, 1):
            lhs = x_buf[xi(ab, whose, h)].reshape(256, H)

            total = jnp.dot(lhs, wx[ab * 2 + whose], preferred_element_type=F32)
            total = total.reshape(2, NZ, R, H)
            if whose == 1:
                total += part[h * 2 + ab]
            part[h * 2 + ab] = total

    up, down = {}, {}

    def chunk(q):
        return q // 4, q // 2 % 2, pl.ds(q % 2 * HALF, HALF)

    def chain_sem(q, way, step):
        return R_CHAIN + q * 4 + way * 2 + step % 2

    def reduce_step(q, s):
        h, p, c = chunk(q)
        if s > 0:
            up[q, s - 1].wait_recv()
            down[q, s - 1].wait_recv()
        for way, hops, send_buf, recv_buf, device in ((0, up, sp, rp, zp), (1, down, sm, rm, zm)):
            first = way
            owner = (z + 4 - s) % NZ if way == 0 else (z + 4 + s) % NZ
            for ab in (0, 1):
                if s == 0 and ab != first:
                    continue
                v = part[h * 2 + ab, p, owner, :, c]
                if s > 1 or (s == 1 and ab == first):
                    v = v + dec(recv_buf[q * 4 + s - 1, ab])
                send_buf[q * 4 + s, ab] = enc(v)
            which = pl.ds(first, 1) if s == 0 else pl.ds(0, 2)
            hops[q, s] = remote(
                send_buf.at[q * 4 + s, which], recv_buf.at[q * 4 + s, which], device,
                S_CHAIN, chain_sem(q, way, s),
            )

    fwd, bwd = {}, {}

    def to_sibling(q, owner):
        if q % 2 == 1:
            t = q // 2
            remote(
                g_buf.at[pl.ds(0, 2), t, owner], g_buf.at[pl.ds(2, 2), t, owner], sib,
                S_PAIR, R_PAIR + t,
            )

    def finish(q):
        h, p, c = chunk(q)
        up[q, 3].wait_recv()
        down[q, 3].wait_recv()
        both = [
            part[h * 2 + ab, p, z, :, c] + dec(rp[q * 4 + 3, ab]) + dec(rm[q * 4 + 3, ab])
            for ab in (0, 1)
        ]
        bias = bias_buf[...].astype(F32).reshape(1, 2 * H)
        bias = jnp.where(core == 0, bias[:, :H], bias[:, H:])[:, q % 2 * HALF : (q % 2 + 1) * HALF]
        value, slope = gelu_parts(both[0] + bias)
        g_buf[0, q // 2, z, :, c] = (both[1] * slope).astype(BF16)
        g_buf[1, q // 2, z, :, c] = value.astype(BF16)
        slot = g_buf.at[pl.ds(0, 2), q // 2, z, :, c]
        fwd[q, 0] = remote(slot, slot, zp, S_CHAIN, chain_sem(q, 0, 0))
        bwd[q, 0] = remote(slot, slot, zm, S_CHAIN, chain_sem(q, 1, 0))
        to_sibling(q, z)

    def spread_step(q, s):
        c = chunk(q)[2]
        fwd[q, s - 1].wait_recv()
        bwd[q, s - 1].wait_recv()
        owners = ((z + NZ - s) % NZ, (z + s) % NZ)
        for i, hops, device in ((0, fwd, zp), (1, bwd, zm)):
            which = pl.ds(i, 1) if s == 3 else pl.ds(0, 2)
            slot = g_buf.at[which, q // 2, owners[i], :, c]
            hops[q, s] = remote(slot, slot, device, S_CHAIN, chain_sem(q, i, s))
        for owner in owners:
            to_sibling(q, owner)

    def spread_last(q):
        fwd[q, 3].wait_recv()
        bwd[q, 3].wait_recv()
        to_sibling(q, (z + 4) % NZ)

    def spread_done(t):
        wait_for(g_buf.at[pl.ds(0, 2), t], recv_sem.at[R_PAIR + t])

    def backproject(h):
        grads = [g_buf[half * 2, pl.ds(2 * h, 2)].reshape(256, H) for half in (0, 1)]
        nt = (((1,), (1,)), ((), ()))

        total = lax.dot_general(grads[0], wx[0], nt, preferred_element_type=F32)
        total += lax.dot_general(grads[1], wu_other[...], nt, preferred_element_type=F32)
        ig_acc[h] = total.reshape(2, 4, 2, R, H)

    halves = (pl.ds(0, HALF), pl.ds(HALF, HALF))

    def rows_for(h, side, k):
        if side == 0:
            yk = (y + k) % 4
            return ig_acc[h, yk % 2, :, yk // 2, :, halves[0]]
        return ig_acc[h, :, (x + k) % 4, :, :, halves[1]].reshape(4, R, HALF)

    def scatter1(h):
        for k in (2, 1, 3):
            for side in (0, 1):
                i = (h * 2 + side) * 3 + k - 1
                s1[i] = enc(rows_for(h, side, k))
                remote(
                    s1.at[i], r1.at[i], (ypeer, xpeer)[side](k), S_NEAR, R_NEAR + h * 2 + side
                )

    def scatter2(h):
        for side in (0, 1):
            total = rows_for(h, side, 0)
            wait_for(r1.at[pl.ds(0, 3)], recv_sem.at[R_NEAR + h * 2 + side])
            for k in (1, 3, 2):
                total = total + dec(r1[(h * 2 + side) * 3 + k - 1])
            t1[h * 2 + side] = total
            for k in (2, 1, 3):
                i = (h * 2 + side) * 3 + k - 1
                if side == 0:
                    block = t1[h * 2, (x + k) % 4]
                else:
                    yk = (y + k) % 4
                    block = t1[h * 2 + 1, (yk % 2) * 2 + yk // 2]
                s2[i] = enc(block)
                remote(
                    s2.at[i], r2.at[i], (xpeer, ypeer)[side](k), S_FAR, R_FAR + h * 2 + side
                )

    def scatter3(h):
        for side in (0, 1):
            total = t1[h * 2, x] if side == 0 else t1[h * 2 + 1, par * 2 + yh]
            wait_for(r2.at[pl.ds(0, 3)], recv_sem.at[R_FAR + h * 2 + side])
            for k in (1, 3, 2):
                total = total + dec(r2[(h * 2 + side) * 3 + k - 1])
            ig_out[pl.ds(h * R, R), halves[side]] = total.astype(BF16)

    def weight_grad(arr, half):
        tokens = x_buf[pl.ds(xi(arr, 0, 0), 2)].reshape(512, H)
        grads = g_buf[half * 2 + arr].reshape(512, H)
        tn = (((0,), (0,)), ((), ()))
        total = lax.dot_general(tokens, grads, tn, preferred_element_type=F32)
        (up_out, down_out)[arr][half] = total.astype(BF16)

    def bias_grad():
        own, other = [
            jnp.sum(g_buf[i].reshape(512, H).astype(F32), axis=0, keepdims=True) for i in (0, 2)
        ]
        left, right = jnp.where(core == 0, own, other), jnp.where(core == 0, other, own)
        bias_out[...] = jnp.concatenate([left, right], axis=1).reshape(2 * H)

    def drain():
        for ref, i in (
            (x_buf.at[0, :, pl.ds(0, 3)], S_GATHER1),
            (x_buf.at[pl.ds(0, 3)], S_GATHER2),
            (x_buf.at[pl.ds(0, 4)], S_SHARE),
            (wx.at[pl.ds(0, 2)], S_WEIGHTS),
            (g_buf.at[:, :, pl.ds(0, 7)], S_CHAIN),
            (g_buf.at[pl.ds(0, 2)], S_PAIR),
            (s1, S_NEAR),
            (s2, S_FAR),
        ):
            wait_for(ref, send_sem.at[i])

    gather1(0)
    gather1(1)
    send_weights()
    gather2(0)
    gather3(0, 1)
    gather2(1)
    gather3(0, 3, 2)
    own_weights_ready()
    project(0, 0)
    weights_ready()
    gathered(0)
    project(0, 1)
    for q in range(4):
        reduce_step(q, 0)
    gather3(1, 1, 3, 2)
    for q in range(4):
        reduce_step(q, 1)
    project(1, 0)
    gathered(1)
    project(1, 1)
    for q in range(4):
        reduce_step(4 + q, 0)
    for q in range(4):
        reduce_step(q, 2)
    for q in range(4):
        reduce_step(4 + q, 1)
    for q in range(4):
        reduce_step(q, 3)
    for q in range(4):
        reduce_step(4 + q, 2)
    for q in range(4):
        finish(q)
    for q in range(4):
        reduce_step(4 + q, 3)
    for q in range(4):
        spread_step(q, 1)
    for q in range(4):
        finish(4 + q)
    for q in range(4):
        spread_step(q, 2)
    for q in range(4):
        spread_step(4 + q, 1)
    for q in range(4):
        spread_step(q, 3)
    for q in range(4):
        spread_step(4 + q, 2)
    for q in range(4):
        spread_last(q)
    for q in range(4):
        spread_step(4 + q, 3)
    spread_done(0)
    spread_done(1)
    backproject(0)
    scatter1(0)
    for q in range(4):
        spread_last(4 + q)
    weight_grad(0, 0)
    spread_done(2)
    spread_done(3)
    backproject(1)
    scatter1(1)
    scatter2(0)
    weight_grad(0, 1)
    weight_grad(1, 0)
    scatter2(1)
    weight_grad(1, 1)
    bias_grad()
    scatter3(0)
    scatter3(1)
    drain()


def place_kernel(up_ref, down_ref, bias_ref, ig_ref, up_hbm, down_hbm, bias_hbm, ig_hbm, sem):
    core = lax.axis_index("row") % 2
    copies = [
        pltpu.make_async_copy(bias_ref, bias_hbm, sem.at[4]),
        pltpu.make_async_copy(ig_ref, ig_hbm, sem.at[5]),
    ]
    for half in (0, 1):
        start = pl.multiple_of((core if half == 0 else 1 - core) * H, H)
        for arr, src, dst in ((0, up_ref, up_hbm), (1, down_ref, down_hbm)):
            cols = dst.at[:, pl.ds(start, H)]
            copies.append(pltpu.make_async_copy(src.at[half], cols, sem.at[half * 2 + arr]))
    for copy in copies:
        copy.start()
    for copy in copies:
        copy.wait()


def body(activations, output_grad, up_weight, down_weight, up_bias):
    anywhere = pl.BlockSpec(memory_space=pl.ANY)
    hbm = pl.BlockSpec(memory_space=pltpu.HBM)
    vmem = pl.BlockSpec(memory_space=pltpu.VMEM)
    operands = [
        pltpu.with_memory_space_constraint(a, pltpu.HBM)
        for a in (activations, output_grad, up_weight, down_weight, up_bias)
    ]
    results = pl.pallas_call(
        exchange_kernel,
        out_shape=[
            pltpu.VMEM((2, H, H), BF16),
            pltpu.VMEM((2, H, H), BF16),
            pltpu.VMEM((2 * H,), F32),
            pltpu.VMEM((2 * R, H), BF16),
        ],
        in_specs=[hbm] * 5,
        out_specs=[vmem] * 4,
        scratch_shapes=[
            pltpu.VMEM((8, 2, 4, 2, R, H), BF16),
            pltpu.VMEM((4, H, H), BF16),
            pltpu.VMEM((H, H), BF16),
            pltpu.VMEM((4, 2, NZ, R, H), F32),
            pltpu.VMEM((32, 2, R, HALF), BF16),
            pltpu.VMEM((32, 2, R, HALF), BF16),
            pltpu.VMEM((32, 2, R, HALF), BF16),
            pltpu.VMEM((32, 2, R, HALF), BF16),
            pltpu.VMEM((4, 4, NZ, R, H), BF16),
            pltpu.VMEM((2, 2, 4, 2, R, H), F32),
            pltpu.VMEM((12, 4, R, HALF), BF16),
            pltpu.VMEM((12, 4, R, HALF), BF16),
            pltpu.VMEM((4, 4, R, HALF), F32),
            pltpu.VMEM((12, R, HALF), BF16),
            pltpu.VMEM((12, R, HALF), BF16),
            pltpu.VMEM((2 * H,), BF16),
            pltpu.SemaphoreType.DMA((N_SEND,)),
            pltpu.SemaphoreType.DMA((N_RECV,)),
            pltpu.SemaphoreType.DMA((N_LOCAL,)),
        ],
        compiler_params=pltpu.CompilerParams(
            collective_id=0, has_side_effects=True, vmem_limit_bytes=44 << 20
        ),
        cost_estimate=pl.CostEstimate(
            flops=5 * 2 * 512 * H * 2 * H, bytes_accessed=12 << 20, transcendentals=64 * H
        ),
        name="exchange",
    )(*operands)
    up_grad, down_grad, bias_grad, input_grad = pl.pallas_call(
        place_kernel,
        out_shape=[
            jax.ShapeDtypeStruct((H, 2 * H), BF16),
            jax.ShapeDtypeStruct((H, 2 * H), BF16),
            jax.ShapeDtypeStruct((2 * H,), F32),
            jax.ShapeDtypeStruct((2 * R, H), BF16),
        ],
        in_specs=[anywhere] * 4,
        out_specs=[hbm] * 4,
        scratch_shapes=[pltpu.SemaphoreType.DMA((6,))],
        compiler_params=pltpu.CompilerParams(vmem_limit_bytes=1 << 20),
        cost_estimate=pl.CostEstimate(flops=0, bytes_accessed=5 << 20, transcendentals=0),
        name="place",
    )(*results)
    return (input_grad, up_grad, down_grad, bias_grad)


def solution(mesh):
    placed = (P("col", "row"), P("col", "row"), P("row", "col"), P("row", "col"), P("col"))
    return jax.shard_map(
        body,
        mesh=mesh,
        in_specs=placed,
        out_specs=(P("col", "row"), P("row", "col"), P("row", "col"), P("col")),
        check_vma=False,
    )
```

```python
import functools

import jax
import jax.numpy as jnp
from jax import lax
from jax.experimental import pallas as pl
from jax.experimental.pallas import tpu as pltpu
from jax.sharding import PartitionSpec as P

MESH = pl.DeviceIdType.MESH
F32 = jnp.float32
BF16 = jnp.bfloat16

NZ = 8
R = 16
H = 768
HALF = H // 2

S_GATHER1, S_GATHER2, S_SHARE, S_WEIGHTS, S_CHAIN, S_PAIR, S_NEAR, S_FAR, N_SEND = range(9)
R_GATHER1, R_GATHER2, R_SHARE, R_WEIGHTS, R_CHAIN, R_PAIR, R_NEAR, R_FAR, N_RECV = (
    0, 2, 14, 16, 17, 49, 53, 57, 61,
)
L_IN, L_UP, L_DOWN, L_OTHER, L_BIAS, N_LOCAL = 0, 2, 3, 4, 5, 6


def gelu_parts(pre_act):
    coeff = 0.7978845608028654
    cubic = 0.044715
    inner = coeff * (pre_act + cubic * pre_act * pre_act * pre_act)
    tanh_val = jnp.tanh(inner)
    value = 0.5 * pre_act * (1.0 + tanh_val)
    slope = 0.5 * (1.0 + tanh_val) + 0.5 * pre_act * (1.0 - tanh_val * tanh_val) * coeff * (
        1.0 + 3.0 * cubic * pre_act * pre_act
    )
    return (value, slope)


def enc(v):
    return (v * jnp.abs(v)).astype(BF16)


def dec(code):
    v = code.astype(F32)
    root = jnp.sqrt(jnp.abs(v))
    return jnp.where(v < 0, -root, root)


def exchange_kernel(
    act_hbm, og_hbm, wu_hbm, wd_hbm, bias_hbm,
    up_out, down_out, bias_out, ig_out,
    x_buf, wx, wu_other, part, sp, rp, sm, rm, g_buf, ig_acc,
    s1, r1, t1, s2, r2, bias_buf, send_sem, recv_sem, local_sem,
):
    row, col = lax.axis_index("row"), lax.axis_index("col")
    z, core = row // 2, row % 2
    x, y = col // 4, col % 4
    par, yh = y % 2, y // 2

    sib = (z * 2 + 1 - core, col)
    zp = (((z + 1) % NZ) * 2 + core, col)
    zm = (((z + NZ - 1) % NZ) * 2 + core, col)

    def xpeer(k):
        return (row, ((x + k) % 4) * 4 + y)

    def ypeer(k):
        return (row, x * 4 + (y + k) % 4)

    def remote(src, dst, device, sent, received):
        copy = pltpu.make_async_remote_copy(
            src_ref=src, dst_ref=dst, send_sem=send_sem.at[sent], recv_sem=recv_sem.at[received],
            device_id=device, device_id_type=MESH,
        )
        copy.start()
        return copy

    def move(src, dst, i):
        copy = pltpu.make_async_copy(src, dst, local_sem.at[i])
        copy.start()
        return copy

    def wait_for(ref, sem):
        pltpu.make_async_copy(ref, ref, sem).wait()

    own_cols = pl.ds(pl.multiple_of(core * H, H), H)
    other_cols = pl.ds(pl.multiple_of((1 - core) * H, H), H)

    def xi(arr, whose, h):
        return arr * 4 + whose * 2 + h

    for h in range(2):
        for arr, src in ((0, act_hbm), (1, og_hbm)):
            move(src.at[pl.ds(h * R, R)], x_buf.at[xi(arr, 0, h), par, x, yh], L_IN + h)
    weights = [
        move(wu_hbm.at[:, own_cols], wx.at[0], L_UP),
        move(wd_hbm.at[:, own_cols], wx.at[2], L_DOWN),
        move(wu_hbm.at[:, other_cols], wu_other, L_OTHER),
        move(bias_hbm, bias_buf, L_BIAS),
    ]

    barrier = pltpu.get_barrier_semaphore()
    peers = [sib, zp, zm] + [xpeer(k) for k in (1, 2, 3)] + [ypeer(k) for k in (1, 2, 3)]
    for peer in peers:
        pl.semaphore_signal(barrier, inc=1, device_id=peer, device_id_type=MESH)
    pl.semaphore_wait(barrier, len(peers))

    stage2 = {}

    def gather1(h):
        wait_for(x_buf.at[0, 0, 0], local_sem.at[L_IN + h])
        for k in (2, 1, 3):
            for arr, peer in ((0, xpeer(k)), (1, ypeer(k))):
                slot = x_buf.at[xi(arr, 0, h), par, x, yh]
                remote(slot, slot, peer, S_GATHER1, R_GATHER1 + h)

    def group(arr, whose, h, k):
        if arr == 0:
            yk = (y + 4 - k) % 4
            return x_buf.at[xi(0, whose, h), yk % 2, :, yk // 2]
        return x_buf.at[xi(1, whose, h), :, (x + 4 - k) % 4]

    def share(arr, h, k):
        remote(group(arr, 0, h, k), group(arr, 1, h, k), sib, S_SHARE, R_SHARE + h)

    def gather2(h):
        wait_for(x_buf.at[0, 0, pl.ds(0, 3)], recv_sem.at[R_GATHER1 + h])
        for k in (2, 1, 3):
            for arr, peer in ((0, ypeer(k)), (1, xpeer(k))):
                slot = group(arr, 0, h, 0)
                i = R_GATHER2 + (h * 2 + arr) * 3 + k - 1
                stage2[arr, h, k] = remote(slot, slot, peer, S_GATHER2, i)
        for arr in (0, 1):
            share(arr, h, 0)

    def gather3(h, *hops):
        for k in hops:
            for arr in (0, 1):
                stage2[arr, h, k].wait_recv()
                share(arr, h, k)

    def gathered(h):
        wait_for(x_buf.at[pl.ds(0, 2)], recv_sem.at[R_SHARE + h])

    def send_weights():
        remote(wu_hbm.at[:, other_cols], wx.at[1], sib, S_WEIGHTS, R_WEIGHTS)
        remote(wd_hbm.at[:, other_cols], wx.at[3], sib, S_WEIGHTS, R_WEIGHTS)

    def own_weights_ready():
        for copy in weights:
            copy.wait()

    def weights_ready():
        wait_for(wx.at[pl.ds(0, 2)], recv_sem.at[R_WEIGHTS])

    def project(h, whose):
        for ab in (0, 1):
            lhs = x_buf[xi(ab, whose, h)].reshape(256, H)

            total = jnp.dot(lhs, wx[ab * 2 + whose], preferred_element_type=F32)
            total = total.reshape(2, NZ, R, H)
            if whose == 1:
                total += part[h * 2 + ab]
            part[h * 2 + ab] = total

    up, down = {}, {}

    def chunk(q):
        return q // 4, q // 2 % 2, pl.ds(q % 2 * HALF, HALF)

    def chain_sem(q, way, step):
        return R_CHAIN + q * 4 + way * 2 + step % 2

    def reduce_step(q, s):
        h, p, c = chunk(q)
        if s > 0:
            up[q, s - 1].wait_recv()
            down[q, s - 1].wait_recv()
        for way, hops, send_buf, recv_buf, device in ((0, up, sp, rp, zp), (1, down, sm, rm, zm)):
            first = way
            owner = (z + 4 - s) % NZ if way == 0 else (z + 4 + s) % NZ
            for ab in (0, 1):
                if s == 0 and ab != first:
                    continue
                v = part[h * 2 + ab, p, owner, :, c]
                if s > 1 or (s == 1 and ab == first):
                    v = v + dec(recv_buf[q * 4 + s - 1, ab])
                send_buf[q * 4 + s, ab] = enc(v)
            which = pl.ds(first, 1) if s == 0 else pl.ds(0, 2)
            hops[q, s] = remote(
                send_buf.at[q * 4 + s, which], recv_buf.at[q * 4 + s, which], device,
                S_CHAIN, chain_sem(q, way, s),
            )

    fwd, bwd = {}, {}

    def to_sibling(q, owner):
        if q % 2 == 1:
            t = q // 2
            remote(
                g_buf.at[pl.ds(0, 2), t, owner], g_buf.at[pl.ds(2, 2), t, owner], sib,
                S_PAIR, R_PAIR + t,
            )

    def finish(q):
        h, p, c = chunk(q)
        up[q, 3].wait_recv()
        down[q, 3].wait_recv()
        both = [
            part[h * 2 + ab, p, z, :, c] + dec(rp[q * 4 + 3, ab]) + dec(rm[q * 4 + 3, ab])
            for ab in (0, 1)
        ]
        bias = bias_buf[...].astype(F32).reshape(1, 2 * H)
        bias = jnp.where(core == 0, bias[:, :H], bias[:, H:])[:, q % 2 * HALF : (q % 2 + 1) * HALF]
        value, slope = gelu_parts(both[0] + bias)
        g_buf[0, q // 2, z, :, c] = (both[1] * slope).astype(BF16)
        g_buf[1, q // 2, z, :, c] = value.astype(BF16)
        slot = g_buf.at[pl.ds(0, 2), q // 2, z, :, c]
        fwd[q, 0] = remote(slot, slot, zp, S_CHAIN, chain_sem(q, 0, 0))
        bwd[q, 0] = remote(slot, slot, zm, S_CHAIN, chain_sem(q, 1, 0))
        to_sibling(q, z)

    def spread_step(q, s):
        c = chunk(q)[2]
        fwd[q, s - 1].wait_recv()
        bwd[q, s - 1].wait_recv()
        owners = ((z + NZ - s) % NZ, (z + s) % NZ)
        for i, hops, device in ((0, fwd, zp), (1, bwd, zm)):
            which = pl.ds(i, 1) if s == 3 else pl.ds(0, 2)
            slot = g_buf.at[which, q // 2, owners[i], :, c]
            hops[q, s] = remote(slot, slot, device, S_CHAIN, chain_sem(q, i, s))
        for owner in owners:
            to_sibling(q, owner)

    def spread_last(q):
        fwd[q, 3].wait_recv()
        bwd[q, 3].wait_recv()
        to_sibling(q, (z + 4) % NZ)

    def spread_done(t):
        wait_for(g_buf.at[pl.ds(0, 2), t], recv_sem.at[R_PAIR + t])

    def backproject(h, half):
        grads = g_buf[half * 2, pl.ds(2 * h, 2)].reshape(256, H)
        weight = (wx.at[0], wu_other)[half][...]
        nt = (((1,), (1,)), ((), ()))
        total = lax.dot_general(grads, weight, nt, preferred_element_type=F32)
        total = total.reshape(2, 4, 2, R, H)
        if half == 1:
            total += ig_acc[h]
        ig_acc[h] = total

    halves = (pl.ds(0, HALF), pl.ds(HALF, HALF))

    def rows_for(h, side, k):
        if side == 0:
            yk = (y + k) % 4
            return ig_acc[h, yk % 2, :, yk // 2, :, halves[0]]
        return ig_acc[h, :, (x + k) % 4, :, :, halves[1]].reshape(4, R, HALF)

    def scatter1(h):
        for k in (2, 1, 3):
            for side in (0, 1):
                i = (h * 2 + side) * 3 + k - 1
                s1[i] = enc(rows_for(h, side, k))
                remote(
                    s1.at[i], r1.at[i], (ypeer, xpeer)[side](k), S_NEAR, R_NEAR + h * 2 + side
                )

    def scatter2(h):
        for side in (0, 1):
            total = rows_for(h, side, 0)
            wait_for(r1.at[pl.ds(0, 3)], recv_sem.at[R_NEAR + h * 2 + side])
            for k in (1, 3, 2):
                total = total + dec(r1[(h * 2 + side) * 3 + k - 1])
            t1[h * 2 + side] = total
            for k in (2, 1, 3):
                i = (h * 2 + side) * 3 + k - 1
                if side == 0:
                    block = t1[h * 2, (x + k) % 4]
                else:
                    yk = (y + k) % 4
                    block = t1[h * 2 + 1, (yk % 2) * 2 + yk // 2]
                s2[i] = enc(block)
                remote(
                    s2.at[i], r2.at[i], (xpeer, ypeer)[side](k), S_FAR, R_FAR + h * 2 + side
                )

    def scatter3(h):
        for side in (0, 1):
            total = t1[h * 2, x] if side == 0 else t1[h * 2 + 1, par * 2 + yh]
            wait_for(r2.at[pl.ds(0, 3)], recv_sem.at[R_FAR + h * 2 + side])
            for k in (1, 3, 2):
                total = total + dec(r2[(h * 2 + side) * 3 + k - 1])
            ig_out[pl.ds(h * R, R), halves[side]] = total.astype(BF16)

    def weight_grad(arr, half):
        tokens = x_buf[pl.ds(xi(arr, 0, 0), 2)].reshape(512, H)
        grads = g_buf[half * 2 + arr].reshape(512, H)
        tn = (((0,), (0,)), ((), ()))
        total = lax.dot_general(tokens, grads, tn, preferred_element_type=F32)
        (up_out, down_out)[arr][half] = total.astype(BF16)

    def bias_grad():
        own, other = [
            jnp.sum(g_buf[i].reshape(512, H).astype(F32), axis=0, keepdims=True) for i in (0, 2)
        ]
        left, right = jnp.where(core == 0, own, other), jnp.where(core == 0, other, own)
        bias_out[...] = jnp.concatenate([left, right], axis=1).reshape(2 * H)

    def drain():
        for ref, i in (
            (x_buf.at[0, :, pl.ds(0, 3)], S_GATHER1),
            (x_buf.at[pl.ds(0, 3)], S_GATHER2),
            (x_buf.at[pl.ds(0, 4)], S_SHARE),
            (wx.at[pl.ds(0, 2)], S_WEIGHTS),
            (g_buf.at[:, :, pl.ds(0, 7)], S_CHAIN),
            (g_buf.at[pl.ds(0, 2)], S_PAIR),
            (s1, S_NEAR),
            (s2, S_FAR),
        ):
            wait_for(ref, send_sem.at[i])

    gather1(0)
    gather1(1)
    send_weights()
    gather2(0)
    gather3(0, 1)
    gather2(1)
    gather3(0, 3, 2)
    own_weights_ready()
    project(0, 0)
    weights_ready()
    gathered(0)
    project(0, 1)
    for q in range(4):
        reduce_step(q, 0)
    gather3(1, 1, 3, 2)
    for q in range(4):
        reduce_step(q, 1)
    project(1, 0)
    gathered(1)
    project(1, 1)
    for q in range(4):
        reduce_step(4 + q, 0)
    for q in range(4):
        reduce_step(q, 2)
    for q in range(4):
        reduce_step(4 + q, 1)
    for q in range(4):
        reduce_step(q, 3)
    for q in range(4):
        reduce_step(4 + q, 2)
    for q in range(4):
        finish(q)
    for q in range(4):
        reduce_step(4 + q, 3)
    for q in range(4):
        spread_step(q, 1)
    for q in range(4):
        finish(4 + q)
    for q in range(4):
        spread_step(q, 2)
    for q in range(4):
        spread_step(4 + q, 1)
    for q in range(4):
        spread_step(q, 3)
    for q in range(4):
        spread_step(4 + q, 2)
    for q in range(4):
        spread_last(q)
    for q in range(4):
        spread_step(4 + q, 3)
    spread_done(0)
    spread_done(1)
    backproject(0, 0)
    backproject(0, 1)
    scatter1(0)
    for q in range(4):
        spread_last(4 + q)
    backproject(1, 0)
    weight_grad(0, 0)
    spread_done(2)
    spread_done(3)
    backproject(1, 1)
    scatter1(1)
    scatter2(0)
    weight_grad(0, 1)
    weight_grad(1, 0)
    scatter2(1)
    weight_grad(1, 1)
    bias_grad()
    scatter3(0)
    scatter3(1)
    drain()


def place_kernel(up_ref, down_ref, bias_ref, ig_ref, up_hbm, down_hbm, bias_hbm, ig_hbm, sem):
    core = lax.axis_index("row") % 2
    copies = [
        pltpu.make_async_copy(bias_ref, bias_hbm, sem.at[4]),
        pltpu.make_async_copy(ig_ref, ig_hbm, sem.at[5]),
    ]
    for half in (0, 1):
        start = pl.multiple_of((core if half == 0 else 1 - core) * H, H)
        for arr, src, dst in ((0, up_ref, up_hbm), (1, down_ref, down_hbm)):
            cols = dst.at[:, pl.ds(start, H)]
            copies.append(pltpu.make_async_copy(src.at[half], cols, sem.at[half * 2 + arr]))
    for copy in copies:
        copy.start()
    for copy in copies:
        copy.wait()


def body(activations, output_grad, up_weight, down_weight, up_bias):
    anywhere = pl.BlockSpec(memory_space=pl.ANY)
    hbm = pl.BlockSpec(memory_space=pltpu.HBM)
    vmem = pl.BlockSpec(memory_space=pltpu.VMEM)
    operands = [
        pltpu.with_memory_space_constraint(a, pltpu.HBM)
        for a in (activations, output_grad, up_weight, down_weight, up_bias)
    ]
    results = pl.pallas_call(
        exchange_kernel,
        out_shape=[
            pltpu.VMEM((2, H, H), BF16),
            pltpu.VMEM((2, H, H), BF16),
            pltpu.VMEM((2 * H,), F32),
            pltpu.VMEM((2 * R, H), BF16),
        ],
        in_specs=[hbm] * 5,
        out_specs=[vmem] * 4,
        scratch_shapes=[
            pltpu.VMEM((8, 2, 4, 2, R, H), BF16),
            pltpu.VMEM((4, H, H), BF16),
            pltpu.VMEM((H, H), BF16),
            pltpu.VMEM((4, 2, NZ, R, H), F32),
            pltpu.VMEM((32, 2, R, HALF), BF16),
            pltpu.VMEM((32, 2, R, HALF), BF16),
            pltpu.VMEM((32, 2, R, HALF), BF16),
            pltpu.VMEM((32, 2, R, HALF), BF16),
            pltpu.VMEM((4, 4, NZ, R, H), BF16),
            pltpu.VMEM((2, 2, 4, 2, R, H), F32),
            pltpu.VMEM((12, 4, R, HALF), BF16),
            pltpu.VMEM((12, 4, R, HALF), BF16),
            pltpu.VMEM((4, 4, R, HALF), F32),
            pltpu.VMEM((12, R, HALF), BF16),
            pltpu.VMEM((12, R, HALF), BF16),
            pltpu.VMEM((2 * H,), BF16),
            pltpu.SemaphoreType.DMA((N_SEND,)),
            pltpu.SemaphoreType.DMA((N_RECV,)),
            pltpu.SemaphoreType.DMA((N_LOCAL,)),
        ],
        compiler_params=pltpu.CompilerParams(
            collective_id=0, has_side_effects=True, vmem_limit_bytes=44 << 20
        ),
        cost_estimate=pl.CostEstimate(
            flops=5 * 2 * 512 * H * 2 * H, bytes_accessed=12 << 20, transcendentals=64 * H
        ),
        name="exchange",
    )(*operands)
    up_grad, down_grad, bias_grad, input_grad = pl.pallas_call(
        place_kernel,
        out_shape=[
            jax.ShapeDtypeStruct((H, 2 * H), BF16),
            jax.ShapeDtypeStruct((H, 2 * H), BF16),
            jax.ShapeDtypeStruct((2 * H,), F32),
            jax.ShapeDtypeStruct((2 * R, H), BF16),
        ],
        in_specs=[anywhere] * 4,
        out_specs=[hbm] * 4,
        scratch_shapes=[pltpu.SemaphoreType.DMA((6,))],
        compiler_params=pltpu.CompilerParams(vmem_limit_bytes=1 << 20),
        cost_estimate=pl.CostEstimate(flops=0, bytes_accessed=5 << 20, transcendentals=0),
        name="place",
    )(*results)
    return (input_grad, up_grad, down_grad, bias_grad)


def solution(mesh):
    placed = (P("col", "row"), P("col", "row"), P("row", "col"), P("row", "col"), P("col"))
    return jax.shard_map(
        body,
        mesh=mesh,
        in_specs=placed,
        out_specs=(P("col", "row"), P("row", "col"), P("row", "col"), P("col")),
        check_vma=False,
    )
```
